512 devices in a mesh: bias: 8 (over z_lo, x), gx: 8 (over z_hi, core), gy: 8 (over y).
Axes of the slice: x: 4, y: 8, z: 8 (z_hi: 4, z_lo: 2; z = z_hi * 2 + z_lo), core: 2. Of those that a mesh axis runs over, the one named last changes fastest.
Arguments:
- source: bfloat16 [8, 16, 24, 32, 256], P('bias', 'gx', 'gy'), may hold values from -6 to 6
- inverse: bfloat16 [8, 16, 24, 256, 256], P('bias', 'gx', 'gy'), may hold values from -0.375 to 0.375
- coupling: bfloat16 [8, 16, 24, 4, 256, 256], P('bias', 'gx', 'gy'), may hold values from -0.1875 to 0.1875
- sensitivity: float32 [8, 16, 24, 256], P('bias', 'gx', 'gy'), may hold values from -6 to 6
Outputs:
- adjoint_out: bfloat16 [8, 16, 24, 32, 256], P('bias', 'gx', 'gy')
- doping_grad: float32 [16, 24, 2048], P('gx', 'gy', 'bias')
The draws below stay inside these ranges and needn't reach their ends.
All inputs are finite; a program needn't handle non-finite values.
Results may differ from the reference program's by a relative error of at most 0.02.
Values may be sent and summed in bfloat16 or wider, within the bound.
A program may use at most 64 MiB of HBM per device.

```python
import jax
import jax.numpy as jnp
from jax import lax

BCELL = 64
VARS = 4
UNK = 256
RHS = 32
ITERS = 3
NBIAS = 8
GBX = 16
GBY = 24


def shard_levels(key, extent, shards, low, largest):
    gain, own = 1.0, jax.random.fold_in(key, 6)
    for position, blocks in shards:
        draws = jnp.exp(jax.random.uniform(jax.random.fold_in(own, position), (blocks,), jnp.float32, low / len(shards), largest / len(shards)))
        gain = gain * jnp.repeat(draws, extent[position] // blocks).reshape([-1 if axis == position else 1 for axis in range(len(extent))])
    return gain


def bell_draw(stream_key, dims, spread, most, shards=(), kind=jnp.bfloat16):
    loudness = shard_levels(stream_key, dims, shards, -0.22, 0.18) if shards else 1.0
    array = jax.random.normal(stream_key, dims, jnp.float32) * spread * loudness
    return jnp.minimum(jnp.maximum(array, -most), most).astype(kind)


def setup_inputs(seed: int = 0) -> dict:
    keys = jax.random.split(jax.random.key(seed), 5)
    source = bell_draw(keys[0], (NBIAS, GBX, GBY, RHS, UNK), 1.0, 6.0, ((0, 8), (1, 8), (2, 8)))
    inverse = bell_draw(keys[1], (NBIAS, GBX, GBY, UNK, UNK), UNK ** -0.5, 0.375, ((0, 8), (1, 8), (2, 8)))
    coupling = bell_draw(keys[2], (NBIAS, GBX, GBY, 4, UNK, UNK), (4 * UNK) ** -0.5, 0.1875, ((0, 8), (1, 8), (2, 8)))
    sensitivity = bell_draw(keys[3], (NBIAS, GBX, GBY, UNK), 1.0, 6.0, ((0, 8), (1, 8), (2, 8)), jnp.float32)
    return {"source": source, "inverse": inverse, "coupling": coupling, "sensitivity": sensitivity}


def one_bias(packed):
    source, inverse, coupling = packed
    source_f = source.astype(jnp.float32)
    inverse_f = inverse.astype(jnp.float32)
    coupling_f = coupling.astype(jnp.float32)
    adjoint = jnp.einsum('xyru,xyuv->xyrv', source_f, inverse_f).astype(jnp.bfloat16)
    for step in range(ITERS):
        products = jnp.einsum('xyru,xyduv->xydrv', adjoint.astype(jnp.float32), coupling_f).astype(jnp.bfloat16)
        padded = jnp.pad(products, ((1, 1), (1, 1), (0, 0), (0, 0), (0, 0))).astype(jnp.float32)
        incoming = padded[:-2, 1:-1, 0] + padded[2:, 1:-1, 1] + padded[1:-1, :-2, 2] + padded[1:-1, 2:, 3]
        update = (source_f - incoming).astype(jnp.bfloat16)
        adjoint = jnp.einsum('xyru,xyuv->xyrv', update.astype(jnp.float32), inverse_f).astype(jnp.bfloat16)
    return adjoint


def reference(source, inverse, coupling, sensitivity):
    adjoint_out = lax.map(one_bias, (source, inverse, coupling))
    shaped = adjoint_out.astype(jnp.float32).reshape(NBIAS, GBX, GBY, RHS, VARS, BCELL)
    weights = sensitivity.reshape(NBIAS, GBX, GBY, 1, VARS, BCELL)
    doping_grad = jnp.sum(shaped * weights, axis=(0, 4)).reshape(GBX, GBY, RHS * BCELL)
    return adjoint_out, doping_grad
```

```python
import jax
import jax.numpy as jnp
from jax import lax
from jax.experimental import pallas as pl
from jax.experimental.pallas import tpu as pltpu
from jax.sharding import PartitionSpec as P

ITERS = 3
BX, BY = 2, 3
BLOCKS = BX * BY
RHS, UNK = 32, 256
PEERS = 8
MESH = pl.DeviceIdType.MESH


def mm(a, b):
    return jnp.dot(a, b, preferred_element_type=jnp.float32)


def kernel(src_h, inv_h, cp_h, sen_h, adj_out, dop_out,
           src, inv, cp, sen, xs, xr, ys, yr, gs, gr,
           lsem, isem, csem, xsend, xrecv, ysend, yrecv, gsend, grecv):
    bias, gx, gy = lax.axis_index("bias"), lax.axis_index("gx"), lax.axis_index("gy")
    nb, nx, ny = lax.axis_size("bias"), lax.axis_size("gx"), lax.axis_size("gy")
    xdev = (lax.rem(gx + nx - 1, nx), lax.rem(gx + 1, nx))
    ydev = (lax.rem(gy + ny - 1, ny), lax.rem(gy + 1, ny))

    barrier = pltpu.get_barrier_semaphore()
    for side in range(2):
        pl.semaphore_signal(barrier, inc=1, device_id={"gx": xdev[side]}, device_id_type=MESH)
        pl.semaphore_signal(barrier, inc=1, device_id={"gy": ydev[side]}, device_id_type=MESH)
    for step in range(1, PEERS):
        pl.semaphore_signal(barrier, inc=1, device_id={"bias": lax.rem(bias + step, nb)}, device_id_type=MESH)

    src_c = pltpu.make_async_copy(src_h, src, lsem.at[0])
    sen_c = pltpu.make_async_copy(sen_h, sen, lsem.at[1])
    src_c.start()
    inv_c = []
    for k in range(BLOCKS):
        c = pltpu.make_async_copy(inv_h.at[k], inv.at[k], isem.at[k])
        c.start()
        inv_c.append(c)
    first = [(j, 1) for j in range(BY)] + [(BY + j, 0) for j in range(BY)]
    first += [(0, 3), (BY, 3), (BY - 1, 2), (2 * BY - 1, 2)]
    rest = [(k, d) for k in range(BLOCKS) for d in range(4) if (k, d) not in first]
    cp_c = {}
    for k, d in first + rest:
        c = pltpu.make_async_copy(cp_h.at[k, d], cp.at[k, d], csem.at[k, d])
        c.start()
        cp_c[k, d] = c
    sen_c.start()

    has_x = (gx > 0, gx < nx - 1)
    has_y = (gy > 0, gy < ny - 1)

    src_c.wait()
    a = []
    for k in range(BLOCKS):
        inv_c[k].wait()
        a.append(mm(src[k], inv[k]).astype(jnp.bfloat16))

    sent = []
    for t in range(ITERS):
        if t == 0:
            for key in first:
                cp_c[key].wait()
        for j in range(BY):
            xs[t, 0, j] = mm(a[j], cp[j, 1]).astype(jnp.bfloat16)
            xs[t, 1, j] = mm(a[BY + j], cp[BY + j, 0]).astype(jnp.bfloat16)
        if t == 0:
            pl.semaphore_wait(barrier, 4 + PEERS - 1)
        for j in range(BY):
            for side in range(2):
                c = pltpu.make_async_remote_copy(
                    src_ref=xs.at[t, side, j], dst_ref=xr.at[t, 1 - side, j],
                    send_sem=xsend.at[t, side, j], recv_sem=xrecv.at[t, 1 - side, j],
                    device_id={"gx": xdev[side]}, device_id_type=MESH)
                c.start()
                sent.append(c)
        for i in range(BX):
            ys[t, 0, i] = mm(a[i * BY], cp[i * BY, 3]).astype(jnp.bfloat16)
            ys[t, 1, i] = mm(a[i * BY + BY - 1], cp[i * BY + BY - 1, 2]).astype(jnp.bfloat16)
        for i in range(BX):
            for side in range(2):
                c = pltpu.make_async_remote_copy(
                    src_ref=ys.at[t, side, i], dst_ref=yr.at[t, 1 - side, i],
                    send_sem=ysend.at[t, side, i], recv_sem=yrecv.at[t, 1 - side, i],
                    device_id={"gy": ydev[side]}, device_id_type=MESH)
                c.start()
                sent.append(c)
        if t == 0:
            for key in rest:
                cp_c[key].wait()
        acc = []
        for k in range(BLOCKS):
            i, j = divmod(k, BY)
            total = src[k].astype(jnp.float32)
            if i > 0:
                total = total - mm(a[k - BY], cp[k - BY, 0])
            if i < BX - 1:
                total = total - mm(a[k + BY], cp[k + BY, 1])
            if j > 0:
                total = total - mm(a[k - 1], cp[k - 1, 2])
            if j < BY - 1:
                total = total - mm(a[k + 1], cp[k + 1, 3])
            acc.append(total)
        for side in range(2):
            for i in range(BX):
                pltpu.make_async_copy(yr.at[t, side, i], yr.at[t, side, i], yrecv.at[t, side, i]).wait()
        for j in range(BY):
            for side in range(2):
                pltpu.make_async_copy(xr.at[t, side, j], xr.at[t, side, j], xrecv.at[t, side, j]).wait()
        new = []
        for k in range(BLOCKS):
            i, j = divmod(k, BY)
            total = acc[k]
            if i == 0:
                total = total - jnp.where(has_x[0], xr[t, 0, j].astype(jnp.float32), 0.0)
            if i == BX - 1:
                total = total - jnp.where(has_x[1], xr[t, 1, j].astype(jnp.float32), 0.0)
            if j == 0:
                total = total - jnp.where(has_y[0], yr[t, 0, i].astype(jnp.float32), 0.0)
            if j == BY - 1:
                total = total - jnp.where(has_y[1], yr[t, 1, i].astype(jnp.float32), 0.0)
            new.append(mm(total.astype(jnp.bfloat16), inv[k]).astype(jnp.bfloat16))
        a = new

    for k in range(BLOCKS):
        adj_out[k] = a[k]

    sen_c.wait()
    lane = lax.broadcasted_iota(jnp.int32, (RHS, 128), 1)
    staged = []
    for k in range(BLOCKS):
        i, j = divmod(k, BY)
        w = sen[j, pl.ds(i, 1), :]
        v = a[k].astype(jnp.float32) * w
        h = v[:, :128] + v[:, 128:]
        h = h + pltpu.roll(h, 64, 1)
        staged.append(jnp.where(lane < 64, h, pltpu.roll(h, RHS - 1, 0)).astype(jnp.bfloat16))
    rows = jnp.concatenate(staged, axis=0)
    r = lax.broadcasted_iota(jnp.int32, (PEERS * 16, BLOCKS * RHS), 0)
    c = lax.broadcasted_iota(jnp.int32, (PEERS * 16, BLOCKS * RHS), 1)
    place = lax.rem(r, 8)
    block = lax.rem(place, 2) * BY + lax.div(place, 2)
    wanted = jnp.where(place < BLOCKS, block * RHS + 2 * lax.div(r, 8), -1)
    pick = jnp.where(c == wanted, 1.0, 0.0).astype(jnp.bfloat16)
    gs[...] = mm(pick, rows).astype(jnp.bfloat16).reshape(PEERS, 16, 128)
    for step in range(1, PEERS):
        peer = lax.rem(bias + step, nb)
        c = pltpu.make_async_remote_copy(
            src_ref=gs.at[peer], dst_ref=gr.at[step], send_sem=gsend.at[step], recv_sem=grecv.at[step],
            device_id={"bias": peer}, device_id_type=MESH)
        c.start()
        sent.append(c)
    total = gs[bias].astype(jnp.float32)
    for step in range(1, PEERS):
        pltpu.make_async_copy(gr.at[step], gr.at[step], grecv.at[step]).wait()
        total = total + gr[step].astype(jnp.float32)
    for j in range(BY):
        dop_out[j, :, :128] = total[2 * j:2 * j + 2]
        dop_out[j, :, 128:] = total[8 + 2 * j:10 + 2 * j]
    for c in sent:
        c.wait_send()


def shards(source, inverse, coupling, sensitivity):
    src = source.reshape(BLOCKS, RHS, UNK)
    inv = inverse.reshape(BLOCKS, UNK, UNK)
    cp = coupling.reshape(BLOCKS, 4, UNK, UNK)
    sen = sensitivity.reshape(BX, BY, UNK).transpose(1, 0, 2)
    hbm = pl.BlockSpec(memory_space=pltpu.HBM)
    dma = pltpu.SemaphoreType.DMA
    adjoint, doping = pl.pallas_call(
        kernel,
        out_shape=(jax.ShapeDtypeStruct((BLOCKS, RHS, UNK), jnp.bfloat16),
                   jax.ShapeDtypeStruct((BY, BX, UNK), jnp.float32)),
        in_specs=[hbm] * 4,
        out_specs=(pl.BlockSpec(memory_space=pltpu.VMEM),) * 2,
        scratch_shapes=[
            pltpu.VMEM((BLOCKS, RHS, UNK), jnp.bfloat16),
            pltpu.VMEM((BLOCKS, UNK, UNK), jnp.bfloat16),
            pltpu.VMEM((BLOCKS, 4, UNK, UNK), jnp.bfloat16),
            pltpu.VMEM((BY, BX, UNK), jnp.float32),
            pltpu.VMEM((ITERS, 2, BY, RHS, UNK), jnp.bfloat16),
            pltpu.VMEM((ITERS, 2, BY, RHS, UNK), jnp.bfloat16),
            pltpu.VMEM((ITERS, 2, BX, RHS, UNK), jnp.bfloat16),
            pltpu.VMEM((ITERS, 2, BX, RHS, UNK), jnp.bfloat16),
            pltpu.VMEM((PEERS, 16, 128), jnp.bfloat16),
            pltpu.VMEM((PEERS, 16, 128), jnp.bfloat16),
            dma((2,)), dma((BLOCKS,)), dma((BLOCKS, 4)),
            dma((ITERS, 2, BY)), dma((ITERS, 2, BY)), dma((ITERS, 2, BX)), dma((ITERS, 2, BX)),
            dma((PEERS,)), dma((PEERS,)),
        ],
        compiler_params=pltpu.CompilerParams(
            collective_id=0, has_side_effects=True, vmem_limit_bytes=40 * 1024 * 1024),
        cost_estimate=pl.CostEstimate(flops=403_000_000, bytes_accessed=4_200_000, transcendentals=0),
    )(*(pltpu.with_memory_space_constraint(x, pltpu.HBM) for x in (src, inv, cp, sen)))
    return (adjoint.reshape(1, BX, BY, RHS, UNK), doping.transpose(1, 0, 2))


def solution(mesh):
    placed = (
        P("bias", "gx", "gy", None, None),
        P("bias", "gx", "gy", None, None),
        P("bias", "gx", "gy", None, None, None),
        P("bias", "gx", "gy", None),
    )
    return jax.shard_map(
        shards,
        mesh=mesh,
        in_specs=placed,
        out_specs=(P("bias", "gx", "gy", None, None), P("gx", "gy", "bias")),
        check_vma=False,
    )
```

```python
import jax
import jax.numpy as jnp
from jax import lax
from jax.experimental import pallas as pl
from jax.experimental.pallas import tpu as pltpu
from jax.sharding import PartitionSpec as P

ITERS = 3
BX, BY = 2, 3
BLOCKS = BX * BY
RHS, UNK = 32, 256
PEERS = 8
MESH = pl.DeviceIdType.MESH


def mm(a, b):
    return jnp.dot(a, b, preferred_element_type=jnp.float32)


def whole(ref, sem):
    return pltpu.make_async_copy(ref, ref, sem)


def kernel(src_h, inv_h, cp_h, sen_h, adj_out, dop_out,
           src, inv, cp, sen, a, acc, zs, zr, cs, cr, ys, yr, gs, gr,
           lsem, ssem, zsem, csem, ysem, gsem):
    bias, gx, gy = lax.axis_index("bias"), lax.axis_index("gx"), lax.axis_index("gy")
    nb, nx, ny = lax.axis_size("bias"), lax.axis_size("gx"), lax.axis_size("gy")
    odd = lax.rem(gx, 2)
    far, near = odd * BY, (1 - odd) * BY
    zdev = {"gx": lax.rem(gx + nx + 2 * odd - 1, nx)}
    cdev = {"gx": gx + 1 - 2 * odd}
    ydev = ({"gy": lax.rem(gy + ny - 1, ny)}, {"gy": lax.rem(gy + 1, ny)})
    has_z = jnp.logical_and(gx + 2 * odd - 1 >= 0, gx + 2 * odd - 1 < nx)
    has_y = (gy > 0, gy < ny - 1)

    pltpu.make_async_copy(src_h, src, lsem.at[0]).start()
    pltpu.make_async_copy(inv_h, inv, lsem.at[1]).start()
    for j in range(BY):
        k = far + j
        pltpu.make_async_copy(cp_h.at[4 * k + 1 - odd], cp.at[4 * k + 1 - odd], lsem.at[2]).start()
    edge_y = [(i * BY + side * (BY - 1), 3 - side) for side in range(2) for i in range(BX)]
    for k, d in edge_y:
        pltpu.make_async_copy(cp_h.at[4 * k + d], cp.at[4 * k + d], lsem.at[3]).start()
    for j in range(BY):
        k = near + j
        pltpu.make_async_copy(cp_h.at[4 * k + odd], cp.at[4 * k + odd], lsem.at[4]).start()
    pltpu.make_async_copy(sen_h, sen, lsem.at[5]).start()

    barrier = pltpu.get_barrier_semaphore()
    for dev in (zdev, cdev) + ydev:
        pl.semaphore_signal(barrier, inc=1, device_id=dev, device_id_type=MESH)
    for step in range(1, PEERS):
        pl.semaphore_signal(barrier, inc=1, device_id={"bias": lax.rem(bias + step, nb)}, device_id_type=MESH)

    whole(src, lsem.at[0]).wait()
    whole(inv, lsem.at[1]).wait()
    inner = [(j, 0) for j in range(BY)] + [(BY + j, 1) for j in range(BY)]
    inner += [(i * BY + j, 2) for i in range(BX) for j in range(BY - 1)]
    inner += [(i * BY + j, 3) for i in range(BX) for j in range(1, BY)]
    for k, d in inner:
        pltpu.make_async_copy(cp_h.at[4 * k + d], cp.at[4 * k + d], lsem.at[6]).start()
    for k in range(BLOCKS):
        a[k] = mm(src[k], inv[k]).astype(jnp.bfloat16)

    for t in range(ITERS):
        if t == 0:
            whole(cp.at[pl.ds(0, BY)], lsem.at[2]).wait()
        for j in range(BY):
            zs[t, j] = mm(a[far + j], cp[4 * (far + j) + 1 - odd]).astype(jnp.bfloat16)
        if t == 0:
            pl.semaphore_wait(barrier, 4 + PEERS - 1)
        for j in range(BY):
            pltpu.make_async_remote_copy(
                src_ref=zs.at[t, j], dst_ref=zr.at[t, j], send_sem=ssem.at[0], recv_sem=zsem.at[t, j],
                device_id=zdev, device_id_type=MESH).start()
        if t == 0:
            whole(cp.at[pl.ds(0, 2 * BX)], lsem.at[3]).wait()
        for side in range(2):
            for i in range(BX):
                k, d = edge_y[side * BX + i]
                ys[t, side, i] = mm(a[k], cp[4 * k + d]).astype(jnp.bfloat16)
        for side in range(2):
            pltpu.make_async_remote_copy(
                src_ref=ys.at[t, side], dst_ref=yr.at[t, 1 - side], send_sem=ssem.at[1], recv_sem=ysem.at[t, 1 - side],
                device_id=ydev[side], device_id_type=MESH).start()
        if t == 0:
            whole(cp.at[pl.ds(0, BY)], lsem.at[4]).wait()
        for j in range(BY):
            cs[t, j] = mm(a[near + j], cp[4 * (near + j) + odd]).astype(jnp.bfloat16)
        pltpu.make_async_remote_copy(
            src_ref=cs.at[t], dst_ref=cr.at[t], send_sem=ssem.at[2], recv_sem=csem.at[t],
            device_id=cdev, device_id_type=MESH).start()
        if t == 0:
            whole(cp.at[pl.ds(0, len(inner))], lsem.at[6]).wait()
        for k in range(BLOCKS):
            i, j = divmod(k, BY)
            total = src[k].astype(jnp.float32)
            if i > 0:
                total = total - mm(a[k - BY], cp[4 * (k - BY)])
            if i < BX - 1:
                total = total - mm(a[k + BY], cp[4 * (k + BY) + 1])
            if j > 0:
                total = total - mm(a[k - 1], cp[4 * (k - 1) + 2])
            if j < BY - 1:
                total = total - mm(a[k + 1], cp[4 * (k + 1) + 3])
            acc[k] = total
        whole(cr.at[t], csem.at[t]).wait()
        near_u = [acc[near + j] - cr[t, j].astype(jnp.float32) for j in range(BY)]
        a[near + 1] = mm(near_u[1].astype(jnp.bfloat16), inv[near + 1]).astype(jnp.bfloat16)
        for side in range(2):
            whole(yr.at[t, side], ysem.at[t, side]).wait()
        for side in range(2):
            j = side * (BY - 1)
            u = near_u[j] - jnp.where(has_y[side], yr[t, side, 1 - odd].astype(jnp.float32), 0.0)
            a[near + j] = mm(u.astype(jnp.bfloat16), inv[near + j]).astype(jnp.bfloat16)
        far_u = [acc[far + j] for j in range(BY)]
        for side in range(2):
            j = side * (BY - 1)
            far_u[j] = far_u[j] - jnp.where(has_y[side], yr[t, side, odd].astype(jnp.float32), 0.0)
        for j in range(BY):
            whole(zr.at[t, j], zsem.at[t, j]).wait()
        for j in range(BY):
            u = far_u[j] - jnp.where(has_z, zr[t, j].astype(jnp.float32), 0.0)
            a[far + j] = mm(u.astype(jnp.bfloat16), inv[far + j]).astype(jnp.bfloat16)

    whole(sen, lsem.at[5]).wait()
    lane = lax.broadcasted_iota(jnp.int32, (RHS, 128), 1)
    staged = []
    for k in range(BLOCKS):
        i, j = divmod(k, BY)
        w = sen[j, pl.ds(i, 1), :]
        v = a[k].astype(jnp.float32) * w
        h = v[:, :128] + v[:, 128:]
        h = h + pltpu.roll(h, 64, 1)
        staged.append(jnp.where(lane < 64, h, pltpu.roll(h, RHS - 1, 0)).astype(jnp.bfloat16))
    rows = jnp.concatenate(staged, axis=0)
    r = lax.broadcasted_iota(jnp.int32, (PEERS * 16, BLOCKS * RHS), 0)
    c = lax.broadcasted_iota(jnp.int32, (PEERS * 16, BLOCKS * RHS), 1)
    place = lax.rem(r, 8)
    block = lax.rem(place, 2) * BY + lax.div(place, 2)
    wanted = jnp.where(place < BLOCKS, block * RHS + 2 * lax.div(r, 8), -1)
    pick = jnp.where(c == wanted, 1.0, 0.0).astype(jnp.bfloat16)
    gs[...] = mm(pick, rows).astype(jnp.bfloat16).reshape(PEERS, 16, 128)
    for step in (6, 2, 5, 7, 1, 3, 4):
        peer = lax.rem(bias + step, nb)
        pltpu.make_async_remote_copy(
            src_ref=gs.at[peer], dst_ref=gr.at[step - 1], send_sem=ssem.at[3], recv_sem=gsem,
            device_id={"bias": peer}, device_id_type=MESH).start()
    adj_out[...] = a[...]
    total = gs[bias].astype(jnp.float32)
    whole(gr, gsem).wait()
    for step in range(1, PEERS):
        total = total + gr[step - 1].astype(jnp.float32)
    for j in range(BY):
        dop_out[j, :, :128] = total[2 * j:2 * j + 2]
        dop_out[j, :, 128:] = total[8 + 2 * j:10 + 2 * j]
    whole(zs, ssem.at[0]).wait()
    whole(ys, ssem.at[1]).wait()
    whole(cs, ssem.at[2]).wait()
    whole(gs.at[pl.ds(0, PEERS - 1)], ssem.at[3]).wait()


def shards(source, inverse, coupling, sensitivity):
    src = source.reshape(BLOCKS, RHS, UNK)
    inv = inverse.reshape(BLOCKS, UNK, UNK)
    cp = coupling.reshape(BLOCKS * 4, UNK, UNK)
    sen = sensitivity.reshape(BX, BY, UNK).transpose(1, 0, 2)
    hbm = pl.BlockSpec(memory_space=pltpu.HBM)
    dma = pltpu.SemaphoreType.DMA
    adjoint, doping = pl.pallas_call(
        kernel,
        out_shape=(jax.ShapeDtypeStruct((BLOCKS, RHS, UNK), jnp.bfloat16),
                   jax.ShapeDtypeStruct((BY, BX, UNK), jnp.float32)),
        in_specs=[hbm] * 4,
        out_specs=(pl.BlockSpec(memory_space=pltpu.VMEM),) * 2,
        scratch_shapes=[
            pltpu.VMEM((BLOCKS, RHS, UNK), jnp.bfloat16),
            pltpu.VMEM((BLOCKS, UNK, UNK), jnp.bfloat16),
            pltpu.VMEM((BLOCKS * 4, UNK, UNK), jnp.bfloat16),
            pltpu.VMEM((BY, BX, UNK), jnp.float32),
            pltpu.VMEM((BLOCKS, RHS, UNK), jnp.bfloat16),
            pltpu.VMEM((BLOCKS, RHS, UNK), jnp.float32),
            pltpu.VMEM((ITERS, BY, RHS, UNK), jnp.bfloat16),
            pltpu.VMEM((ITERS, BY, RHS, UNK), jnp.bfloat16),
            pltpu.VMEM((ITERS, BY, RHS, UNK), jnp.bfloat16),
            pltpu.VMEM((ITERS, BY, RHS, UNK), jnp.bfloat16),
            pltpu.VMEM((ITERS, 2, BX, RHS, UNK), jnp.bfloat16),
            pltpu.VMEM((ITERS, 2, BX, RHS, UNK), jnp.bfloat16),
            pltpu.VMEM((PEERS, 16, 128), jnp.bfloat16),
            pltpu.VMEM((PEERS - 1, 16, 128), jnp.bfloat16),
            dma((7,)), dma((4,)), dma((ITERS, BY)), dma((ITERS,)), dma((ITERS, 2)), dma(()),
        ],
        compiler_params=pltpu.CompilerParams(
            collective_id=0, has_side_effects=True, vmem_limit_bytes=40 * 1024 * 1024),
        cost_estimate=pl.CostEstimate(flops=403_000_000, bytes_accessed=4_200_000, transcendentals=0),
    )(*(pltpu.with_memory_space_constraint(x, pltpu.HBM) for x in (src, inv, cp, sen)))
    return (adjoint.reshape(1, BX, BY, RHS, UNK), doping.transpose(1, 0, 2))


def solution(mesh):
    placed = (
        P("bias", "gx", "gy", None, None),
        P("bias", "gx", "gy", None, None),
        P("bias", "gx", "gy", None, None, None),
        P("bias", "gx", "gy", None),
    )
    return jax.shard_map(
        shards,
        mesh=mesh,
        in_specs=placed,
        out_specs=(P("bias", "gx", "gy", None, None), P("gx", "gy", "bias")),
        check_vma=False,
    )
```

```python
import jax
import jax.numpy as jnp
from jax import lax
from jax.experimental import pallas as pl
from jax.experimental.pallas import tpu as pltpu
from jax.sharding import PartitionSpec as P

ITERS = 3
BX, BY = 2, 3
BLOCKS = BX * BY
RHS, UNK = 32, 256
PEERS = 8
MESH = pl.DeviceIdType.MESH


def mm(a, b):
    return jnp.dot(a, b, preferred_element_type=jnp.float32)


def whole(ref, sem):
    return pltpu.make_async_copy(ref, ref, sem)


def kernel(src_h, inv_h, cp_h, sen_h, adj_out, dop_out,
           src, inv, cp, sen, a, acc, zs, zr, cs, cr, ys, yr, fold, wz, wy, wr, gs, gr,
           lsem, ssem, zsem, csem, ysem, wsem, gsem):
    bias, gx, gy = lax.axis_index("bias"), lax.axis_index("gx"), lax.axis_index("gy")
    nb, nx, ny = lax.axis_size("bias"), lax.axis_size("gx"), lax.axis_size("gy")
    odd = lax.rem(gx, 2)
    far, near = odd * BY, (1 - odd) * BY
    zdev = {"gx": lax.rem(gx + nx + 2 * odd - 1, nx)}
    cdev = {"gx": gx + 1 - 2 * odd}
    ydev = ({"gy": lax.rem(gy + ny - 1, ny)}, {"gy": lax.rem(gy + 1, ny)})
    has_z = jnp.logical_and(gx + 2 * odd - 1 >= 0, gx + 2 * odd - 1 < nx)
    has_y = (gy > 0, gy < ny - 1)
    peers = [lax.rem(bias + step, nb) for step in range(PEERS)]

    def load(from_ref, to_ref, sem):
        pltpu.make_async_copy(from_ref, to_ref, lsem.at[sem]).start()

    def load_tile(k, sem):
        load(cp_h.at[k], cp.at[k], sem)

    def product(k, d):
        return mm(a[k], cp[4 * k + d]).astype(jnp.bfloat16)

    def send(from_ref, to_ref, sent, landed, dev):
        pltpu.make_async_remote_copy(
            src_ref=from_ref, dst_ref=to_ref, send_sem=ssem.at[sent], recv_sem=landed,
            device_id=dev, device_id_type=MESH).start()

    far_rows, near_rows = pl.ds(far, BY), pl.ds(near, BY)
    load(src_h, src, 0)
    load(inv_h.at[far_rows], inv.at[far_rows], 1)
    barrier = pltpu.get_barrier_semaphore()
    for dev in (zdev,) + ydev + (cdev,):
        pl.semaphore_signal(barrier, inc=1, device_id=dev, device_id_type=MESH)
    for j in range(BY):
        load_tile(4 * (far + j) + 1 - odd, 2)
    for peer in peers[1:]:
        pl.semaphore_signal(barrier, inc=1, device_id={"bias": peer}, device_id_type=MESH)
    load(inv_h.at[near_rows], inv.at[near_rows], 3)
    edge_y = [(i * BY + side * (BY - 1), 3 - side) for side in range(2) for i in range(BX)]
    for k, d in edge_y:
        load_tile(4 * k + d, 4)
    for j in range(BY):
        load_tile(4 * (near + j) + odd, 5)
    load(sen_h, sen, 6)

    whole(src, lsem.at[0]).wait()
    whole(inv.at[far_rows], lsem.at[1]).wait()
    for j in range(BY):
        a[far + j] = mm(src[far + j], inv[far + j]).astype(jnp.bfloat16)
    inner = [(j, 0) for j in range(BY)] + [(BY + j, 1) for j in range(BY)]
    inner += [(i * BY + j, 2) for i in range(BX) for j in range(BY - 1)]
    inner += [(i * BY + j, 3) for i in range(BX) for j in range(1, BY)]
    lane_w = lax.broadcasted_iota(jnp.int32, (UNK, 128), 1) < 64
    lane_e = lax.broadcasted_iota(jnp.int32, (RHS, 128), 1) < 64
    lane_g = lax.broadcasted_iota(jnp.int32, (4, 128), 1) < 64

    for t in range(ITERS):
        if t == 0:
            whole(cp.at[pl.ds(0, BY)], lsem.at[2]).wait()
        for j in range(BY):
            zs[t, j] = product(far + j, 1 - odd)
        if t == 0:
            pl.semaphore_wait(barrier, 3 + PEERS)
        for j in range(BY):
            send(zs.at[t, j], zr.at[t, j], 0, zsem.at[t, j], zdev)
        if t == 0:
            for k, d in inner:
                load_tile(4 * k + d, 7)
            whole(inv.at[near_rows], lsem.at[3]).wait()
            for j in range(BY):
                a[near + j] = mm(src[near + j], inv[near + j]).astype(jnp.bfloat16)
            whole(cp.at[pl.ds(0, 2 * BX)], lsem.at[4]).wait()
        for side in range(2):
            for i in range(BX):
                k, d = edge_y[side * BX + i]
                ys[t, side, i] = product(k, d)
        for side in range(2):
            send(ys.at[t, side], yr.at[t, 1 - side], 1, ysem.at[t, 1 - side], ydev[side])
        if t == 0:
            whole(cp.at[pl.ds(0, BY)], lsem.at[5]).wait()
        for j in range(BY):
            cs[t, j] = product(near + j, odd)
        send(cs.at[t], cr.at[t], 2, csem.at[t], cdev)
        if t == ITERS - 1:
            whole(wr, wsem).wait()
            parts = [jnp.where(lane_e, mm(zs[t, 0], wr[0]), mm(zs[t, 1], wr[0])), mm(zs[t, 2], wr[1])]
            for m, part in enumerate(parts):
                for p in range(PEERS):
                    gs[p, m] = part[4 * p:4 * p + 4]
            for step in range(PEERS - 1, -1, -1):
                send(gs.at[peers[step], pl.ds(0, 2)], gr.at[pl.ds(2 * step, 2)], 3, gsem, {"bias": peers[step], **zdev})
            for side in range(2):
                part = jnp.where(lane_e, mm(ys[t, side, 0], wr[2 + side]), mm(ys[t, side, 1], wr[2 + side]))
                for p in range(PEERS):
                    gs[p, 2 + side] = part[4 * p:4 * p + 4]
            for side in range(2):
                for step in range(PEERS - 1, -1, -1):
                    send(gs.at[peers[step], pl.ds(2 + side, 1)], gr.at[pl.ds(16 + 8 * (1 - side) + step, 1)], 3, gsem,
                         {"bias": peers[step], **ydev[side]})
        if t == 0:
            whole(cp.at[pl.ds(0, len(inner))], lsem.at[7]).wait()
        for k in range(BLOCKS):
            i, j = divmod(k, BY)
            total = src[k].astype(jnp.float32)
            if i > 0:
                total = total - mm(a[k - BY], cp[4 * (k - BY)])
            if i < BX - 1:
                total = total - mm(a[k + BY], cp[4 * (k + BY) + 1])
            if j > 0:
                total = total - mm(a[k - 1], cp[4 * (k - 1) + 2])
            if j < BY - 1:
                total = total - mm(a[k + 1], cp[4 * (k + 1) + 3])
            acc[k] = total
        if t == 0:
            whole(sen, lsem.at[6]).wait()
            for k in range(BLOCKS):
                i, j = divmod(k, BY)
                h = inv[k].astype(jnp.float32) * sen[j, i:i + 1, :]
                h = h[:, :128] + h[:, 128:]
                fold[k] = h + pltpu.roll(h, 64, 1)
            for j in range(BY):
                wy[j] = jnp.where(lane_w, fold[j], fold[BY + j]).astype(jnp.bfloat16)
            wz[0] = jnp.where(lane_w, fold[far], fold[far + 1]).astype(jnp.bfloat16)
            wz[1] = fold[far + 2].astype(jnp.bfloat16)
            for side in range(2):
                send(wy.at[side * (BY - 1)], wr.at[3 - side], 4, wsem, ydev[side])
        if t < ITERS - 1:
            send(wz.at[t], wr.at[t], 4, wsem, zdev)
        whole(cr.at[t], csem.at[t]).wait()
        for j in range(BY):
            acc[near + j] = acc[near + j] - cr[t, j].astype(jnp.float32)
        if t == ITERS - 1:
            for j in range(BY):
                part = jnp.where(lane_e, mm(acc[j].astype(jnp.bfloat16), wy[j]), mm(acc[BY + j].astype(jnp.bfloat16), wy[j]))
                for p in range(PEERS):
                    gs[p, 4 + j] = part[4 * p:4 * p + 4]
            for step in (6, 2, 5, 7, 1, 3, 4):
                send(gs.at[peers[step], pl.ds(4, 3)], gr.at[pl.ds(32 + 3 * (step - 1), 3)], 3, gsem, {"bias": peers[step]})
        near_u = [acc[near + j] for j in range(BY)]
        a[near + 1] = mm(near_u[1].astype(jnp.bfloat16), inv[near + 1]).astype(jnp.bfloat16)
        for side in range(2):
            whole(yr.at[t, side], ysem.at[t, side]).wait()
        for side in range(2):
            j = side * (BY - 1)
            u = near_u[j] - jnp.where(has_y[side], yr[t, side, 1 - odd].astype(jnp.float32), 0.0)
            a[near + j] = mm(u.astype(jnp.bfloat16), inv[near + j]).astype(jnp.bfloat16)
        far_u = [acc[far + j] for j in range(BY)]
        for side in range(2):
            j = side * (BY - 1)
            far_u[j] = far_u[j] - jnp.where(has_y[side], yr[t, side, odd].astype(jnp.float32), 0.0)
        for j in range(BY):
            whole(zr.at[t, j], zsem.at[t, j]).wait()
        for j in range(BY):
            u = far_u[j] - jnp.where(has_z, zr[t, j].astype(jnp.float32), 0.0)
            a[far + j] = mm(u.astype(jnp.bfloat16), inv[far + j]).astype(jnp.bfloat16)

    adj_out[...] = a[...]
    whole(zs, ssem.at[0]).wait()
    whole(ys, ssem.at[1]).wait()
    whole(cs, ssem.at[2]).wait()
    whole(wr, ssem.at[4]).wait()
    totals = [gs[bias, 4 + j] for j in range(BY)]
    whole(gr, gsem).wait()
    for step in range(1, PEERS):
        for j in range(BY):
            totals[j] = totals[j] + gr[32 + 3 * (step - 1) + j]
    for side in range(2):
        part = gr[16 + 8 * side]
        for step in range(1, PEERS):
            part = part + gr[16 + 8 * side + step]
        j = side * (BY - 1)
        totals[j] = totals[j] - jnp.where(has_y[side], part, 0.0)
    pair, last = gr[0], gr[1]
    for step in range(1, PEERS):
        pair, last = pair + gr[2 * step], last + gr[2 * step + 1]
    turned = pltpu.roll(pair, 64, 1)
    half = lax.broadcasted_iota(jnp.int32, (4, 128), 1) // 64 == jnp.where(has_z, odd, -1)
    for j, part in enumerate((jnp.where(lane_g, pair, turned), jnp.where(lane_g, turned, pair), last)):
        here = totals[j] - jnp.where(half, part, 0.0)
        other = pltpu.roll(here, 64, 1)
        for q in range(0, 4, 2):
            dop_out[j, 0:1, 64 * q:64 * q + 128] = jnp.where(lane_g[:1], here[q:q + 1], other[q + 1:q + 2])
            dop_out[j, 1:2, 64 * q:64 * q + 128] = jnp.where(lane_g[:1], other[q:q + 1], here[q + 1:q + 2])
    whole(gr, ssem.at[3]).wait()


def shards(source, inverse, coupling, sensitivity):
    src = source.reshape(BLOCKS, RHS, UNK)
    inv = inverse.reshape(BLOCKS, UNK, UNK)
    cp = coupling.reshape(BLOCKS * 4, UNK, UNK)
    sen = sensitivity.reshape(BX, BY, UNK).transpose(1, 0, 2)
    hbm = pl.BlockSpec(memory_space=pltpu.HBM)
    dma = pltpu.SemaphoreType.DMA
    adjoint, doping = pl.pallas_call(
        kernel,
        out_shape=(jax.ShapeDtypeStruct((BLOCKS, RHS, UNK), jnp.bfloat16),
                   jax.ShapeDtypeStruct((BY, BX, UNK), jnp.float32)),
        in_specs=[hbm] * 4,
        out_specs=(pl.BlockSpec(memory_space=pltpu.VMEM),) * 2,
        scratch_shapes=[
            pltpu.VMEM((BLOCKS, RHS, UNK), jnp.bfloat16),
            pltpu.VMEM((BLOCKS, UNK, UNK), jnp.bfloat16),
            pltpu.VMEM((BLOCKS * 4, UNK, UNK), jnp.bfloat16),
            pltpu.VMEM((BY, BX, UNK), jnp.float32),
            pltpu.VMEM((BLOCKS, RHS, UNK), jnp.bfloat16),
            pltpu.VMEM((BLOCKS, RHS, UNK), jnp.float32),
            pltpu.VMEM((ITERS, BY, RHS, UNK), jnp.bfloat16),
            pltpu.VMEM((ITERS, BY, RHS, UNK), jnp.bfloat16),
            pltpu.VMEM((ITERS, BY, RHS, UNK), jnp.bfloat16),
            pltpu.VMEM((ITERS, BY, RHS, UNK), jnp.bfloat16),
            pltpu.VMEM((ITERS, 2, BX, RHS, UNK), jnp.bfloat16),
            pltpu.VMEM((ITERS, 2, BX, RHS, UNK), jnp.bfloat16),
            pltpu.VMEM((BLOCKS, UNK, 128), jnp.float32),
            pltpu.VMEM((2, UNK, 128), jnp.bfloat16),
            pltpu.VMEM((BY, UNK, 128), jnp.bfloat16),
            pltpu.VMEM((4, UNK, 128), jnp.bfloat16),
            pltpu.VMEM((PEERS, 7, 4, 128), jnp.float32),
            pltpu.VMEM((16 + 16 + 3 * (PEERS - 1), 4, 128), jnp.float32),
            dma((8,)), dma((5,)), dma((ITERS, BY)), dma((ITERS,)), dma((ITERS, 2)), dma(()), dma(()),
        ],
        compiler_params=pltpu.CompilerParams(
            collective_id=0, has_side_effects=True, vmem_limit_bytes=40 * 1024 * 1024),
        cost_estimate=pl.CostEstimate(flops=403_000_000, bytes_accessed=4_200_000, transcendentals=0),
    )(*(pltpu.with_memory_space_constraint(x, pltpu.HBM) for x in (src, inv, cp, sen)))
    return (adjoint.reshape(1, BX, BY, RHS, UNK), doping.transpose(1, 0, 2))


def solution(mesh):
    placed = (
        P("bias", "gx", "gy", None, None),
        P("bias", "gx", "gy", None, None),
        P("bias", "gx", "gy", None, None, None),
        P("bias", "gx", "gy", None),
    )
    return jax.shard_map(
        shards,
        mesh=mesh,
        in_specs=placed,
        out_specs=(P("bias", "gx", "gy", None, None), P("gx", "gy", "bias")),
        check_vma=False,
    )
```

```python
import jax
import jax.numpy as jnp
from jax import lax
from jax.experimental import pallas as pl
from jax.experimental.pallas import tpu as pltpu
from jax.sharding import PartitionSpec as P

ITERS = 3
BX, BY = 2, 3
BLOCKS = BX * BY
RHS, UNK = 32, 256
PEERS = 8
MESH = pl.DeviceIdType.MESH


def mm(a, b):
    return jnp.dot(a, b, preferred_element_type=jnp.float32)


def whole(ref, sem):
    return pltpu.make_async_copy(ref, ref, sem)


def kernel(src_h, inv_h, cp_h, sen_h, adj_out, dop_out,
           src, inv, cp, sen, a, acc, zs, zr, cs, cr, ys, yr, both, fold, wz, wy, wr, gs, gr,
           lsem, ssem, zsem, csem, ysem, wsem, gsem, rsem):
    bias, gx, gy = lax.axis_index("bias"), lax.axis_index("gx"), lax.axis_index("gy")
    nb, nx, ny = lax.axis_size("bias"), lax.axis_size("gx"), lax.axis_size("gy")
    odd = lax.rem(gx, 2)
    far, near = odd * BY, (1 - odd) * BY
    zdev = {"gx": lax.rem(gx + nx + 2 * odd - 1, nx)}
    cdev = {"gx": gx + 1 - 2 * odd}
    ydev = ({"gy": lax.rem(gy + ny - 1, ny)}, {"gy": lax.rem(gy + 1, ny)})
    has_z = jnp.logical_and(gx + 2 * odd - 1 >= 0, gx + 2 * odd - 1 < nx)
    has_y = (gy > 0, gy < ny - 1)
    peers = [lax.rem(bias + step, nb) for step in range(PEERS)]

    ring = nb // 2
    place, half = lax.rem(bias, ring), bias - lax.rem(bias, ring)
    round_devs = ({"bias": half + lax.rem(place + 1, ring)}, {"bias": half + lax.rem(place + ring - 1, ring)},
                  {"bias": lax.rem(bias + ring, nb)})

    def tell(number):
        for dev in round_devs:
            pl.semaphore_signal(rsem.at[number], inc=1, device_id=dev, device_id_type=MESH)

    def load(from_ref, to_ref, sem):
        pltpu.make_async_copy(from_ref, to_ref, lsem.at[sem]).start()

    def load_tile(k, sem):
        load(cp_h.at[k], cp.at[k], sem)

    def product(k, d):
        return mm(a[k], cp[4 * k + d]).astype(jnp.bfloat16)

    def send(from_ref, to_ref, sent, landed, dev):
        pltpu.make_async_remote_copy(
            src_ref=from_ref, dst_ref=to_ref, send_sem=ssem.at[sent], recv_sem=landed,
            device_id=dev, device_id_type=MESH).start()

    far_rows, near_rows = pl.ds(far, BY), pl.ds(near, BY)
    load(src_h, src, 0)
    load(inv_h.at[far_rows], inv.at[far_rows], 1)
    barrier = pltpu.get_barrier_semaphore()
    for dev in (zdev,) + ydev + (cdev,):
        pl.semaphore_signal(barrier, inc=1, device_id=dev, device_id_type=MESH)
    for j in range(BY):
        load_tile(4 * (far + j) + 1 - odd, 2)
    for dev in round_devs:
        pl.semaphore_signal(barrier, inc=1, device_id=dev, device_id_type=MESH)
    load(inv_h.at[near_rows], inv.at[near_rows], 3)
    edge_y = [(i * BY + side * (BY - 1), 3 - side) for side in range(2) for i in range(BX)]
    for k, d in edge_y:
        load_tile(4 * k + d, 4)
    for j in range(BY):
        load_tile(4 * (near + j) + odd, 5)
    load(sen_h, sen, 6)

    whole(src, lsem.at[0]).wait()
    whole(inv.at[far_rows], lsem.at[1]).wait()
    for j in range(BY):
        a[far + j] = mm(src[far + j], inv[far + j]).astype(jnp.bfloat16)
    inner = [(j, 0) for j in range(BY)] + [(BY + j, 1) for j in range(BY)]
    inner += [(i * BY + j, 2) for i in range(BX) for j in range(BY - 1)]
    inner += [(i * BY + j, 3) for i in range(BX) for j in range(1, BY)]
    lane_w = lax.broadcasted_iota(jnp.int32, (UNK, 128), 1) < 64
    lane_e = lax.broadcasted_iota(jnp.int32, (RHS, 128), 1) < 64
    lane_g = lax.broadcasted_iota(jnp.int32, (4, 128), 1) < 64

    for t in range(ITERS):
        if t == 0:
            whole(cp.at[pl.ds(0, BY)], lsem.at[2]).wait()
        if t == 0:
            for j in range(BY):
                zs[0, j] = product(far + j, 1 - odd)
            pl.semaphore_wait(barrier, 4 + 3)
            for j in range(BY):
                send(zs.at[0, j], zr.at[0, j], 0, zsem.at[0, j], zdev)
            tell(0)
        if t == 0:
            for k, d in inner:
                load_tile(4 * k + d, 7)
            whole(inv.at[near_rows], lsem.at[3]).wait()
            for j in range(BY):
                a[near + j] = mm(src[near + j], inv[near + j]).astype(jnp.bfloat16)
            whole(cp.at[pl.ds(0, 2 * BX)], lsem.at[4]).wait()
        for side in range(2):
            for i in range(BX):
                k, d = edge_y[side * BX + i]
                ys[t, side, i] = product(k, d)
        if t < ITERS - 1:
            for side in range(2):
                send(ys.at[t, side], yr.at[t, 1 - side], 1, ysem.at[t, 1 - side], ydev[side])
        if t == 0:
            whole(sen, lsem.at[6]).wait()
            for k in range(BLOCKS):
                i, j = divmod(k, BY)
                h = inv[k].astype(jnp.float32) * sen[j, i:i + 1, :]
                h = h[:, :128] + h[:, 128:]
                fold[k] = h + pltpu.roll(h, 64, 1)
            wz[:UNK] = jnp.where(lane_w, fold[far], fold[far + 1]).astype(jnp.bfloat16)
            wz[UNK:] = jnp.where(lane_w[:128], fold[far + 2, :128], fold[far + 2, 128:]).astype(jnp.bfloat16)
            send(wz, wr.at[pl.ds(0, UNK + 128)], 4, wsem, zdev)
            for j in (0, 2, 1):
                wy[j] = jnp.where(lane_w, fold[j], fold[BY + j]).astype(jnp.bfloat16)
            for side in range(2):
                send(wy.at[side * (BY - 1)], wr.at[pl.ds(UNK + 128 + UNK * (1 - side), UNK)], 4, wsem, ydev[side])
            whole(cp.at[pl.ds(0, BY)], lsem.at[5]).wait()
        for j in range(BY):
            cs[t, j] = product(near + j, odd)
        send(cs.at[t], cr.at[t], 2, csem.at[t], cdev)
        if t == ITERS - 1:
            for side in range(2):
                edge = wr[UNK + 128 + UNK * side:2 * UNK + 128 + UNK * side]
                part = jnp.where(lane_e, mm(ys[t, side, 0], edge), mm(ys[t, side, 1], edge))
                for p in range(PEERS):
                    gs[p, 2 + side] = part[4 * p:4 * p + 4]
            for step in (6, 2, 5, 7, 1, 3, 4, 0):
                for side in range(2):
                    send(gs.at[peers[step], pl.ds(2 + side, 1)], gr.at[pl.ds(16 + 8 * (1 - side) + step, 1)], 3, gsem,
                         {"bias": peers[step], **ydev[side]})
            for j in range(BY):
                send(zs.at[t, j], zr.at[t, j], 0, zsem.at[t, j], zdev)
            for side in range(2):
                send(ys.at[t, side], yr.at[t, 1 - side], 1, ysem.at[t, 1 - side], ydev[side])
        if t == 0:
            whole(cp.at[pl.ds(0, len(inner))], lsem.at[7]).wait()
        for k in range(BLOCKS):
            i, j = divmod(k, BY)
            total = src[k].astype(jnp.float32)
            if i > 0:
                total = total - mm(a[k - BY], cp[4 * (k - BY)])
            if i < BX - 1:
                total = total - mm(a[k + BY], cp[4 * (k + BY) + 1])
            if j > 0:
                total = total - mm(a[k - 1], cp[4 * (k - 1) + 2])
            if j < BY - 1:
                total = total - mm(a[k + 1], cp[4 * (k + 1) + 3])
            acc[k] = total
        if t == 0:
            for j in range(BY):
                both[j] = mm(inv[far + j], cp[4 * (far + j) + 1 - odd]).astype(jnp.bfloat16)
            pl.semaphore_wait(rsem.at[0], 3)
            tell(1)
        whole(cr.at[t], csem.at[t]).wait()
        for j in range(BY):
            acc[near + j] = acc[near + j] - cr[t, j].astype(jnp.float32)
        if t == ITERS - 1:
            for j in range(BY):
                part = jnp.where(lane_e, mm(acc[j].astype(jnp.bfloat16), wy[j]), mm(acc[BY + j].astype(jnp.bfloat16), wy[j]))
                for p in range(PEERS):
                    gs[p, 4 + j] = part[4 * p:4 * p + 4]
            for step in (6, 2, 5, 7, 1, 3, 4):
                send(gs.at[peers[step], pl.ds(4, 3)], gr.at[pl.ds(32 + 3 * (step - 1), 3)], 3, gsem, {"bias": peers[step]})
        near_u = [acc[near + j] for j in range(BY)]
        a[near + 1] = mm(near_u[1].astype(jnp.bfloat16), inv[near + 1]).astype(jnp.bfloat16)
        for side in range(2):
            whole(yr.at[t, side], ysem.at[t, side]).wait()
        for side in range(2):
            j = side * (BY - 1)
            u = near_u[j] - jnp.where(has_y[side], yr[t, side, 1 - odd].astype(jnp.float32), 0.0)
            a[near + j] = mm(u.astype(jnp.bfloat16), inv[near + j]).astype(jnp.bfloat16)
        far_u = [acc[far + j] for j in range(BY)]
        for side in range(2):
            j = side * (BY - 1)
            far_u[j] = far_u[j] - jnp.where(has_y[side], yr[t, side, odd].astype(jnp.float32), 0.0)
        for j in range(BY):
            whole(zr.at[t, j], zsem.at[t, j]).wait()
        late = []
        for j in range(BY):
            u = far_u[j] - jnp.where(has_z, zr[t, j].astype(jnp.float32), 0.0)
            late.append(u.astype(jnp.bfloat16))
        if t < ITERS - 1:
            for j in range(BY):
                zs[t + 1, j] = mm(late[j], both[j]).astype(jnp.bfloat16)
            if t == 0:
                pl.semaphore_wait(rsem.at[1], 3)
            if t + 1 < ITERS - 1:
                for j in range(BY):
                    send(zs.at[t + 1, j], zr.at[t + 1, j], 0, zsem.at[t + 1, j], zdev)
            else:
                whole(wr, wsem).wait()
                edge = wr[:UNK]
                tail = wr[UNK:UNK + 128]
                parts = [jnp.where(lane_e, mm(zs[t + 1, 0], edge), mm(zs[t + 1, 1], edge)),
                         mm(zs[t + 1, 2, :, :128], tail) + pltpu.roll(mm(zs[t + 1, 2, :, 128:], tail), 64, 1)]
                for m, part in enumerate(parts):
                    for p in range(PEERS):
                        gs[p, m] = part[4 * p:4 * p + 4]
                for step in (6, 2, 5, 7, 1, 3, 4, 0):
                    send(gs.at[peers[step], pl.ds(0, 2)], gr.at[pl.ds(2 * step, 2)], 3, gsem, {"bias": peers[step], **zdev})
        for j in range(BY):
            a[far + j] = mm(late[j], inv[far + j]).astype(jnp.bfloat16)

    adj_out[...] = a[...]
    whole(zs, ssem.at[0]).wait()
    whole(ys, ssem.at[1]).wait()
    whole(cs, ssem.at[2]).wait()
    whole(wr, ssem.at[4]).wait()
    totals = [gs[bias, 4 + j] for j in range(BY)]
    whole(gr, gsem).wait()
    for step in range(1, PEERS):
        for j in range(BY):
            totals[j] = totals[j] + gr[32 + 3 * (step - 1) + j]
    for side in range(2):
        part = gr[16 + 8 * side]
        for step in range(1, PEERS):
            part = part + gr[16 + 8 * side + step]
        j = side * (BY - 1)
        totals[j] = totals[j] - jnp.where(has_y[side], part, 0.0)
    pair, last = gr[0], gr[1]
    for step in range(1, PEERS):
        pair, last = pair + gr[2 * step], last + gr[2 * step + 1]
    turned = pltpu.roll(pair, 64, 1)
    half = lax.broadcasted_iota(jnp.int32, (4, 128), 1) // 64 == jnp.where(has_z, odd, -1)
    for j, part in enumerate((jnp.where(lane_g, pair, turned), jnp.where(lane_g, turned, pair),
                              jnp.where(lane_g, last, pltpu.roll(last, 64, 1)))):
        here = totals[j] - jnp.where(half, part, 0.0)
        other = pltpu.roll(here, 64, 1)
        for q in range(0, 4, 2):
            dop_out[j, 0:1, 64 * q:64 * q + 128] = jnp.where(lane_g[:1], here[q:q + 1], other[q + 1:q + 2])
            dop_out[j, 1:2, 64 * q:64 * q + 128] = jnp.where(lane_g[:1], other[q:q + 1], here[q + 1:q + 2])
    whole(gr, ssem.at[3]).wait()


def shards(source, inverse, coupling, sensitivity):
    src = source.reshape(BLOCKS, RHS, UNK)
    inv = inverse.reshape(BLOCKS, UNK, UNK)
    cp = coupling.reshape(BLOCKS * 4, UNK, UNK)
    sen = sensitivity.reshape(BX, BY, UNK).transpose(1, 0, 2)
    hbm = pl.BlockSpec(memory_space=pltpu.HBM)
    dma = pltpu.SemaphoreType.DMA
    adjoint, doping = pl.pallas_call(
        kernel,
        out_shape=(jax.ShapeDtypeStruct((BLOCKS, RHS, UNK), jnp.bfloat16),
                   jax.ShapeDtypeStruct((BY, BX, UNK), jnp.float32)),
        in_specs=[hbm] * 4,
        out_specs=(pl.BlockSpec(memory_space=pltpu.VMEM),) * 2,
        scratch_shapes=[
            pltpu.VMEM((BLOCKS, RHS, UNK), jnp.bfloat16),
            pltpu.VMEM((BLOCKS, UNK, UNK), jnp.bfloat16),
            pltpu.VMEM((BLOCKS * 4, UNK, UNK), jnp.bfloat16),
            pltpu.VMEM((BY, BX, UNK), jnp.float32),
            pltpu.VMEM((BLOCKS, RHS, UNK), jnp.bfloat16),
            pltpu.VMEM((BLOCKS, RHS, UNK), jnp.float32),
            pltpu.VMEM((ITERS, BY, RHS, UNK), jnp.bfloat16),
            pltpu.VMEM((ITERS, BY, RHS, UNK), jnp.bfloat16),
            pltpu.VMEM((ITERS, BY, RHS, UNK), jnp.bfloat16),
            pltpu.VMEM((ITERS, BY, RHS, UNK), jnp.bfloat16),
            pltpu.VMEM((ITERS, 2, BX, RHS, UNK), jnp.bfloat16),
            pltpu.VMEM((ITERS, 2, BX, RHS, UNK), jnp.bfloat16),
            pltpu.VMEM((BY, UNK, UNK), jnp.bfloat16),
            pltpu.VMEM((BLOCKS, UNK, 128), jnp.float32),
            pltpu.VMEM((UNK + 128, 128), jnp.bfloat16),
            pltpu.VMEM((BY, UNK, 128), jnp.bfloat16),
            pltpu.VMEM((3 * UNK + 128, 128), jnp.bfloat16),
            pltpu.VMEM((PEERS, 7, 4, 128), jnp.float32),
            pltpu.VMEM((16 + 16 + 3 * (PEERS - 1), 4, 128), jnp.float32),
            dma((8,)), dma((5,)), dma((ITERS, BY)), dma((ITERS,)), dma((ITERS, 2)), dma(()), dma(()), pltpu.SemaphoreType.REGULAR((2,)),
        ],
        compiler_params=pltpu.CompilerParams(
            collective_id=0, has_side_effects=True, vmem_limit_bytes=40 * 1024 * 1024),
        cost_estimate=pl.CostEstimate(flops=403_000_000, bytes_accessed=4_200_000, transcendentals=0),
    )(*(pltpu.with_memory_space_constraint(x, pltpu.HBM) for x in (src, inv, cp, sen)))
    return (adjoint.reshape(1, BX, BY, RHS, UNK), doping.transpose(1, 0, 2))


def solution(mesh):
    placed = (
        P("bias", "gx", "gy", None, None),
        P("bias", "gx", "gy", None, None),
        P("bias", "gx", "gy", None, None, None),
        P("bias", "gx", "gy", None),
    )
    return jax.shard_map(
        shards,
        mesh=mesh,
        in_specs=placed,
        out_specs=(P("bias", "gx", "gy", None, None), P("gx", "gy", "bias")),
        check_vma=False,
    )
```

```python
import jax
import jax.numpy as jnp
from jax import lax
from jax.experimental import pallas as pl
from jax.experimental.pallas import tpu as pltpu
from jax.sharding import PartitionSpec as P

ITERS = 3
BX, BY = 2, 3
BLOCKS = BX * BY
RHS, UNK = 32, 256
PEERS = 8
MESH = pl.DeviceIdType.MESH


def mm(a, b):
    return jnp.dot(a, b, preferred_element_type=jnp.float32)


def whole(ref, sem):
    return pltpu.make_async_copy(ref, ref, sem)


def kernel(src_h, inv_h, cp_h, sen_h, adj_out, dop_out,
           src, inv, cp, sen, a, acc, zs, zr, cs, cr, ys, yr, both, fold, wz, wy, wr, gs, gr,
           lsem, ssem, zsem, csem, ysem, wsem, gsem, rsem):
    bias, gx, gy = lax.axis_index("bias"), lax.axis_index("gx"), lax.axis_index("gy")
    nb, nx, ny = lax.axis_size("bias"), lax.axis_size("gx"), lax.axis_size("gy")
    odd = lax.rem(gx, 2)
    far, near = odd * BY, (1 - odd) * BY
    zdev = {"gx": lax.rem(gx + nx + 2 * odd - 1, nx)}
    cdev = {"gx": gx + 1 - 2 * odd}
    ydev = ({"gy": lax.rem(gy + ny - 1, ny)}, {"gy": lax.rem(gy + 1, ny)})
    has_z = jnp.logical_and(gx + 2 * odd - 1 >= 0, gx + 2 * odd - 1 < nx)
    has_y = (gy > 0, gy < ny - 1)
    peers = [lax.rem(bias + step, nb) for step in range(PEERS)]

    ring = nb // 2
    place, half = lax.rem(bias, ring), bias - lax.rem(bias, ring)
    round_devs = ({"bias": half + lax.rem(place + 1, ring)}, {"bias": half + lax.rem(place + ring - 1, ring)},
                  {"bias": lax.rem(bias + ring, nb)})

    def tell(number):
        for dev in round_devs:
            pl.semaphore_signal(rsem.at[number], inc=1, device_id=dev, device_id_type=MESH)

    def load(from_ref, to_ref, sem):
        pltpu.make_async_copy(from_ref, to_ref, lsem.at[sem]).start()

    def load_tile(k, sem):
        load(cp_h.at[k], cp.at[k], sem)

    def product(k, d):
        return mm(a[k], cp[4 * k + d]).astype(jnp.bfloat16)

    def send(from_ref, to_ref, sent, landed, dev):
        pltpu.make_async_remote_copy(
            src_ref=from_ref, dst_ref=to_ref, send_sem=ssem.at[sent], recv_sem=landed,
            device_id=dev, device_id_type=MESH).start()

    far_rows, near_rows = pl.ds(far, BY), pl.ds(near, BY)
    load(src_h, src, 0)
    load(inv_h.at[far_rows], inv.at[far_rows], 1)
    barrier = pltpu.get_barrier_semaphore()
    for dev in (zdev,) + ydev + (cdev,):
        pl.semaphore_signal(barrier, inc=1, device_id=dev, device_id_type=MESH)
    for j in range(BY):
        load_tile(4 * (far + j) + 1 - odd, 2)
    for dev in round_devs:
        pl.semaphore_signal(barrier, inc=1, device_id=dev, device_id_type=MESH)
    load(inv_h.at[near_rows], inv.at[near_rows], 3)
    edge_y = [(i * BY + side * (BY - 1), 3 - side) for side in range(2) for i in range(BX)]
    for k, d in edge_y:
        load_tile(4 * k + d, 4)
    for j in range(BY):
        load_tile(4 * (near + j) + odd, 5)
    load(sen_h, sen, 6)

    whole(src, lsem.at[0]).wait()
    whole(inv.at[far_rows], lsem.at[1]).wait()
    for j in range(BY):
        a[far + j] = mm(src[far + j], inv[far + j]).astype(jnp.bfloat16)
    inner = [(j, 0) for j in range(BY)] + [(BY + j, 1) for j in range(BY)]
    inner += [(i * BY + j, 2) for i in range(BX) for j in range(BY - 1)]
    inner += [(i * BY + j, 3) for i in range(BX) for j in range(1, BY)]
    lane_w = lax.broadcasted_iota(jnp.int32, (UNK, 128), 1) < 64
    lane_e = lax.broadcasted_iota(jnp.int32, (RHS, 128), 1) < 64
    lane_g = lax.broadcasted_iota(jnp.int32, (4, 128), 1) < 64

    for t in range(ITERS):
        if t == 0:
            whole(cp.at[pl.ds(0, BY)], lsem.at[2]).wait()
        if t == 0:
            for j in range(BY):
                zs[0, j] = product(far + j, 1 - odd)
            pl.semaphore_wait(barrier, 4 + 3)
            send(zs.at[0], zr.at[0], 0, zsem.at[0], zdev)
            tell(0)
        if t == 0:
            for k, d in inner:
                load_tile(4 * k + d, 7)
            whole(inv.at[near_rows], lsem.at[3]).wait()
            for j in range(BY):
                a[near + j] = mm(src[near + j], inv[near + j]).astype(jnp.bfloat16)
            whole(cp.at[pl.ds(0, 2 * BX)], lsem.at[4]).wait()
        for side in range(2):
            for i in range(BX):
                k, d = edge_y[side * BX + i]
                ys[t, side, i] = product(k, d)
        if t < ITERS - 1:
            for side in range(2):
                send(ys.at[t, side], yr.at[t, 1 - side], 1, ysem.at[t], ydev[side])
        if t == 0:
            whole(sen, lsem.at[6]).wait()
            for k in range(BLOCKS):
                i, j = divmod(k, BY)
                h = inv[k].astype(jnp.float32) * sen[j, i:i + 1, :]
                h = h[:, :128] + h[:, 128:]
                fold[k] = h + pltpu.roll(h, 64, 1)
            wz[:UNK] = jnp.where(lane_w, fold[far], fold[far + 1]).astype(jnp.bfloat16)
            wz[UNK:] = jnp.where(lane_w[:128], fold[far + 2, :128], fold[far + 2, 128:]).astype(jnp.bfloat16)
            send(wz, wr.at[pl.ds(0, UNK + 128)], 4, wsem, zdev)
            for j in (0, 2, 1):
                wy[j] = jnp.where(lane_w, fold[j], fold[BY + j]).astype(jnp.bfloat16)
            for side in range(2):
                send(wy.at[side * (BY - 1)], wr.at[pl.ds(UNK + 128 + UNK * (1 - side), UNK)], 4, wsem, ydev[side])
            whole(cp.at[pl.ds(0, BY)], lsem.at[5]).wait()
        for j in range(BY):
            cs[t, j] = product(near + j, odd)
        send(cs.at[t], cr.at[t], 2, csem.at[t], cdev)
        if t == ITERS - 1:
            for side in range(2):
                edge = wr[UNK + 128 + UNK * side:2 * UNK + 128 + UNK * side]
                part = jnp.where(lane_e, mm(ys[t, side, 0], edge), mm(ys[t, side, 1], edge))
                for p in range(PEERS):
                    gs[p, 2 + side] = part[4 * p:4 * p + 4]
            for step in (6, 2, 5, 7, 1, 3, 4, 0):
                for side in range(2):
                    send(gs.at[peers[step], pl.ds(2 + side, 1)], gr.at[pl.ds(16 + 8 * (1 - side) + step, 1)], 3, gsem,
                         {"bias": peers[step], **ydev[side]})
            send(zs.at[t], zr.at[t], 0, zsem.at[t], zdev)
            for side in range(2):
                send(ys.at[t, side], yr.at[t, 1 - side], 1, ysem.at[t], ydev[side])
        if t == 0:
            whole(cp.at[pl.ds(0, len(inner))], lsem.at[7]).wait()
        for k in range(BLOCKS):
            i, j = divmod(k, BY)
            total = src[k].astype(jnp.float32)
            if i > 0:
                total = total - mm(a[k - BY], cp[4 * (k - BY)])
            if i < BX - 1:
                total = total - mm(a[k + BY], cp[4 * (k + BY) + 1])
            if j > 0:
                total = total - mm(a[k - 1], cp[4 * (k - 1) + 2])
            if j < BY - 1:
                total = total - mm(a[k + 1], cp[4 * (k + 1) + 3])
            acc[k] = total
        if t == 0:
            for j in range(BY):
                both[j] = mm(inv[far + j], cp[4 * (far + j) + 1 - odd]).astype(jnp.bfloat16)
            pl.semaphore_wait(rsem.at[0], 3)
            tell(1)
        whole(cr.at[t], csem.at[t]).wait()
        for j in range(BY):
            acc[near + j] = acc[near + j] - cr[t, j].astype(jnp.float32)
        if t == ITERS - 1:
            for j in range(BY):
                part = jnp.where(lane_e, mm(acc[j].astype(jnp.bfloat16), wy[j]), mm(acc[BY + j].astype(jnp.bfloat16), wy[j]))
                for p in range(PEERS):
                    gs[p, 4 + j] = part[4 * p:4 * p + 4]
            for step in (6, 2, 5, 7, 1, 3, 4):
                send(gs.at[peers[step], pl.ds(4, 3)], gr.at[pl.ds(32 + 3 * (step - 1), 3)], 3, gsem, {"bias": peers[step]})
        near_u = [acc[near + j] for j in range(BY)]
        a[near + 1] = mm(near_u[1].astype(jnp.bfloat16), inv[near + 1]).astype(jnp.bfloat16)
        whole(yr.at[t], ysem.at[t]).wait()
        for side in range(2):
            j = side * (BY - 1)
            u = near_u[j] - jnp.where(has_y[side], yr[t, side, 1 - odd].astype(jnp.float32), 0.0)
            a[near + j] = mm(u.astype(jnp.bfloat16), inv[near + j]).astype(jnp.bfloat16)
        far_u = [acc[far + j] for j in range(BY)]
        for side in range(2):
            j = side * (BY - 1)
            far_u[j] = far_u[j] - jnp.where(has_y[side], yr[t, side, odd].astype(jnp.float32), 0.0)
        whole(zr.at[t], zsem.at[t]).wait()
        late = []
        for j in range(BY):
            u = far_u[j] - jnp.where(has_z, zr[t, j].astype(jnp.float32), 0.0)
            late.append(u.astype(jnp.bfloat16))
        if t < ITERS - 1:
            for j in range(BY):
                zs[t + 1, j] = mm(late[j], both[j]).astype(jnp.bfloat16)
            if t == 0:
                pl.semaphore_wait(rsem.at[1], 3)
            if t + 1 < ITERS - 1:
                send(zs.at[t + 1], zr.at[t + 1], 0, zsem.at[t + 1], zdev)
            else:
                whole(wr, wsem).wait()
                edge = wr[:UNK]
                tail = wr[UNK:UNK + 128]
                parts = [jnp.where(lane_e, mm(zs[t + 1, 0], edge), mm(zs[t + 1, 1], edge)),
                         mm(zs[t + 1, 2, :, :128], tail) + pltpu.roll(mm(zs[t + 1, 2, :, 128:], tail), 64, 1)]
                for m, part in enumerate(parts):
                    for p in range(PEERS):
                        gs[p, m] = part[4 * p:4 * p + 4]
                for step in (6, 2, 5, 7, 1, 3, 4, 0):
                    send(gs.at[peers[step], pl.ds(0, 2)], gr.at[pl.ds(2 * step, 2)], 3, gsem, {"bias": peers[step], **zdev})
        for j in range(BY):
            a[far + j] = mm(late[j], inv[far + j]).astype(jnp.bfloat16)

    adj_out[...] = a[...]
    whole(zs, ssem.at[0]).wait()
    whole(ys, ssem.at[1]).wait()
    whole(cs, ssem.at[2]).wait()
    whole(wr, ssem.at[4]).wait()
    totals = [gs[bias, 4 + j] for j in range(BY)]
    whole(gr, gsem).wait()
    for step in range(1, PEERS):
        for j in range(BY):
            totals[j] = totals[j] + gr[32 + 3 * (step - 1) + j]
    for side in range(2):
        part = gr[16 + 8 * side]
        for step in range(1, PEERS):
            part = part + gr[16 + 8 * side + step]
        j = side * (BY - 1)
        totals[j] = totals[j] - jnp.where(has_y[side], part, 0.0)
    pair, last = gr[0], gr[1]
    for step in range(1, PEERS):
        pair, last = pair + gr[2 * step], last + gr[2 * step + 1]
    turned = pltpu.roll(pair, 64, 1)
    half = lax.broadcasted_iota(jnp.int32, (4, 128), 1) // 64 == jnp.where(has_z, odd, -1)
    for j, part in enumerate((jnp.where(lane_g, pair, turned), jnp.where(lane_g, turned, pair),
                              jnp.where(lane_g, last, pltpu.roll(last, 64, 1)))):
        here = totals[j] - jnp.where(half, part, 0.0)
        other = pltpu.roll(here, 64, 1)
        for q in range(0, 4, 2):
            dop_out[j, 0:1, 64 * q:64 * q + 128] = jnp.where(lane_g[:1], here[q:q + 1], other[q + 1:q + 2])
            dop_out[j, 1:2, 64 * q:64 * q + 128] = jnp.where(lane_g[:1], other[q:q + 1], here[q + 1:q + 2])
    whole(gr, ssem.at[3]).wait()


def finish(adj_in, dop_in, adj_out, dop_out, sem):
    first = pltpu.make_async_copy(adj_in, adj_out, sem.at[0])
    second = pltpu.make_async_copy(dop_in, dop_out, sem.at[1])
    first.start()
    second.start()
    first.wait()
    second.wait()


def shards(source, inverse, coupling, sensitivity):
    src = source.reshape(BLOCKS, RHS, UNK)
    inv = inverse.reshape(BLOCKS, UNK, UNK)
    cp = coupling.reshape(BLOCKS * 4, UNK, UNK)
    sen = sensitivity.reshape(BX, BY, UNK).transpose(1, 0, 2)
    hbm = pl.BlockSpec(memory_space=pltpu.HBM)
    dma = pltpu.SemaphoreType.DMA
    adjoint, doping = pl.pallas_call(
        kernel,
        out_shape=(jax.ShapeDtypeStruct((BLOCKS, RHS, UNK), jnp.bfloat16),
                   jax.ShapeDtypeStruct((BY, BX, UNK), jnp.float32)),
        in_specs=[hbm] * 4,
        out_specs=(pl.BlockSpec(memory_space=pltpu.VMEM),) * 2,
        scratch_shapes=[
            pltpu.VMEM((BLOCKS, RHS, UNK), jnp.bfloat16),
            pltpu.VMEM((BLOCKS, UNK, UNK), jnp.bfloat16),
            pltpu.VMEM((BLOCKS * 4, UNK, UNK), jnp.bfloat16),
            pltpu.VMEM((BY, BX, UNK), jnp.float32),
            pltpu.VMEM((BLOCKS, RHS, UNK), jnp.bfloat16),
            pltpu.VMEM((BLOCKS, RHS, UNK), jnp.float32),
            pltpu.VMEM((ITERS, BY, RHS, UNK), jnp.bfloat16),
            pltpu.VMEM((ITERS, BY, RHS, UNK), jnp.bfloat16),
            pltpu.VMEM((ITERS, BY, RHS, UNK), jnp.bfloat16),
            pltpu.VMEM((ITERS, BY, RHS, UNK), jnp.bfloat16),
            pltpu.VMEM((ITERS, 2, BX, RHS, UNK), jnp.bfloat16),
            pltpu.VMEM((ITERS, 2, BX, RHS, UNK), jnp.bfloat16),
            pltpu.VMEM((BY, UNK, UNK), jnp.bfloat16),
            pltpu.VMEM((BLOCKS, UNK, 128), jnp.float32),
            pltpu.VMEM((UNK + 128, 128), jnp.bfloat16),
            pltpu.VMEM((BY, UNK, 128), jnp.bfloat16),
            pltpu.VMEM((3 * UNK + 128, 128), jnp.bfloat16),
            pltpu.VMEM((PEERS, 7, 4, 128), jnp.float32),
            pltpu.VMEM((16 + 16 + 3 * (PEERS - 1), 4, 128), jnp.float32),
            dma((8,)), dma((5,)), dma((ITERS,)), dma((ITERS,)), dma((ITERS,)), dma(()), dma(()), pltpu.SemaphoreType.REGULAR((2,)),
        ],
        compiler_params=pltpu.CompilerParams(
            collective_id=0, has_side_effects=True, vmem_limit_bytes=40 * 1024 * 1024),
        cost_estimate=pl.CostEstimate(flops=403_000_000, bytes_accessed=4_200_000, transcendentals=0),
    )(*(pltpu.with_memory_space_constraint(x, pltpu.HBM) for x in (src, inv, cp, sen)))
    adjoint, doping = pl.pallas_call(
        finish,
        out_shape=(jax.ShapeDtypeStruct((BLOCKS, RHS, UNK), jnp.bfloat16),
                   jax.ShapeDtypeStruct((BY, BX, UNK), jnp.float32)),
        in_specs=[pl.BlockSpec(memory_space=pltpu.VMEM)] * 2,
        out_specs=(pl.BlockSpec(memory_space=pl.ANY),) * 2,
        scratch_shapes=[dma((2,))],
        compiler_params=pltpu.CompilerParams(vmem_limit_bytes=40 * 1024 * 1024),
    )(adjoint, doping)
    return (adjoint.reshape(1, BX, BY, RHS, UNK), doping.transpose(1, 0, 2))


def solution(mesh):
    placed = (
        P("bias", "gx", "gy", None, None),
        P("bias", "gx", "gy", None, None),
        P("bias", "gx", "gy", None, None, None),
        P("bias", "gx", "gy", None),
    )
    return jax.shard_map(
        shards,
        mesh=mesh,
        in_specs=placed,
        out_specs=(P("bias", "gx", "gy", None, None), P("gx", "gy", "bias")),
        check_vma=False,
    )
```

```python
import jax
import jax.numpy as jnp
from jax import lax
from jax.experimental import pallas as pl
from jax.experimental.pallas import tpu as pltpu
from jax.sharding import PartitionSpec as P

ITERS = 3
BX, BY = 2, 3
BLOCKS = BX * BY
RHS, UNK = 32, 256
PEERS = 8
MESH = pl.DeviceIdType.MESH


def mm(a, b):
    return jnp.dot(a, b, preferred_element_type=jnp.float32)


def whole(ref, sem):
    return pltpu.make_async_copy(ref, ref, sem)


def kernel(src_h, inv_h, cp_h, sen_h, adj_out, dop_out,
           src, inv, cp, sen, a, acc, zs, zr, cs, cr, ys, yr, both, fold, wz, wy, wr, gs, gr,
           lsem, ssem, zsem, csem, ysem, wsem, gsem, rsem):
    bias, gx, gy = lax.axis_index("bias"), lax.axis_index("gx"), lax.axis_index("gy")
    nb, nx, ny = lax.axis_size("bias"), lax.axis_size("gx"), lax.axis_size("gy")
    odd = lax.rem(gx, 2)
    far, near = odd * BY, (1 - odd) * BY
    zdev = {"gx": lax.rem(gx + nx + 2 * odd - 1, nx)}
    cdev = {"gx": gx + 1 - 2 * odd}
    ydev = ({"gy": lax.rem(gy + ny - 1, ny)}, {"gy": lax.rem(gy + 1, ny)})
    has_z = jnp.logical_and(gx + 2 * odd - 1 >= 0, gx + 2 * odd - 1 < nx)
    has_y = (gy > 0, gy < ny - 1)
    peers = [lax.rem(bias + step, nb) for step in range(PEERS)]

    ring = nb // 2
    place, half = lax.rem(bias, ring), bias - lax.rem(bias, ring)
    round_devs = ({"bias": half + lax.rem(place + 1, ring)}, {"bias": half + lax.rem(place + ring - 1, ring)},
                  {"bias": lax.rem(bias + ring, nb)})

    def tell(number):
        for dev in round_devs:
            pl.semaphore_signal(rsem.at[number], inc=1, device_id=dev, device_id_type=MESH)

    def load(from_ref, to_ref, sem):
        pltpu.make_async_copy(from_ref, to_ref, lsem.at[sem]).start()

    def load_tile(k, sem):
        load(cp_h.at[k], cp.at[k], sem)

    def product(k, d):
        return mm(a[k], cp[4 * k + d]).astype(jnp.bfloat16)

    def send(from_ref, to_ref, sent, landed, dev):
        pltpu.make_async_remote_copy(
            src_ref=from_ref, dst_ref=to_ref, send_sem=ssem.at[sent], recv_sem=landed,
            device_id=dev, device_id_type=MESH).start()

    def send_z(t):
        @pl.when(has_z)
        def _():
            send(zs.at[t], zr.at[t], 0, zsem.at[t], zdev)

    def send_y(t):
        for side in range(2):
            @pl.when(has_y[side])
            def _():
                send(ys.at[side, t], yr.at[1 - side, t], 3 + side, ysem.at[1 - side, t], ydev[side])

    def wait_if(there, *pairs):
        @pl.when(there)
        def _():
            for ref, sem in pairs:
                whole(ref, sem).wait()

    far_rows, near_rows = pl.ds(far, BY), pl.ds(near, BY)
    load(src_h, src, 0)
    load(inv_h.at[far_rows], inv.at[far_rows], 1)
    barrier = pltpu.get_barrier_semaphore()
    for dev, there in ((zdev, has_z), (ydev[0], has_y[0]), (ydev[1], has_y[1])):
        @pl.when(there)
        def _():
            pl.semaphore_signal(barrier, inc=1, device_id=dev, device_id_type=MESH)
    pl.semaphore_signal(barrier, inc=1, device_id=cdev, device_id_type=MESH)
    greeted = 4 + sum(there.astype(jnp.int32) for there in (has_z,) + has_y)
    for j in range(BY):
        load_tile(4 * (far + j) + 1 - odd, 2)
    for dev in round_devs:
        pl.semaphore_signal(barrier, inc=1, device_id=dev, device_id_type=MESH)
    load(inv_h.at[near_rows], inv.at[near_rows], 3)
    edge_y = [(i * BY + side * (BY - 1), 3 - side) for side in range(2) for i in range(BX)]
    for k, d in edge_y:
        load_tile(4 * k + d, 4)
    for j in range(BY):
        load_tile(4 * (near + j) + odd, 5)
    load(sen_h, sen, 6)

    @pl.when(jnp.logical_not(has_z))
    def _():
        zr[...] = jnp.zeros_like(zr)
        wr[:UNK + 128] = jnp.zeros((UNK + 128, 128), jnp.bfloat16)
        gr[:16] = jnp.zeros((16, 4, 128), jnp.float32)

    for side in range(2):
        @pl.when(jnp.logical_not(has_y[side]))
        def _():
            yr[side] = jnp.zeros((ITERS, BX, RHS, UNK), jnp.bfloat16)
            wr[UNK + 128 + UNK * side:2 * UNK + 128 + UNK * side] = jnp.zeros((UNK, 128), jnp.bfloat16)
            gr[16 + 8 * side:24 + 8 * side] = jnp.zeros((8, 4, 128), jnp.float32)

    whole(src, lsem.at[0]).wait()
    whole(inv.at[far_rows], lsem.at[1]).wait()
    for j in range(BY):
        a[far + j] = mm(src[far + j], inv[far + j]).astype(jnp.bfloat16)
    inner = [(j, 0) for j in range(BY)] + [(BY + j, 1) for j in range(BY)]
    inner += [(i * BY + j, 2) for i in range(BX) for j in range(BY - 1)]
    inner += [(i * BY + j, 3) for i in range(BX) for j in range(1, BY)]
    lane_w = lax.broadcasted_iota(jnp.int32, (UNK, 128), 1) < 64
    lane_e = lax.broadcasted_iota(jnp.int32, (RHS, 128), 1) < 64
    lane_g = lax.broadcasted_iota(jnp.int32, (4, 128), 1) < 64

    for t in range(ITERS):
        if t == 0:
            whole(cp.at[pl.ds(0, BY)], lsem.at[2]).wait()
        if t == 0:
            for j in range(BY):
                zs[0, j] = product(far + j, 1 - odd)
            pl.semaphore_wait(barrier, greeted)
            send_z(0)
            tell(0)
        if t == 0:
            for k, d in inner:
                load_tile(4 * k + d, 7)
            whole(inv.at[near_rows], lsem.at[3]).wait()
            for j in range(BY):
                a[near + j] = mm(src[near + j], inv[near + j]).astype(jnp.bfloat16)
            whole(cp.at[pl.ds(0, 2 * BX)], lsem.at[4]).wait()
        for side in range(2):
            for i in range(BX):
                k, d = edge_y[side * BX + i]
                ys[side, t, i] = product(k, d)
        if t < ITERS - 1:
            send_y(t)
        if t == 0:
            whole(sen, lsem.at[6]).wait()
            for k in range(BLOCKS):
                i, j = divmod(k, BY)
                h = inv[k].astype(jnp.float32) * sen[j, i:i + 1, :]
                h = h[:, :128] + h[:, 128:]
                fold[k] = h + pltpu.roll(h, 64, 1)
            wz[:UNK] = jnp.where(lane_w, fold[far], fold[far + 1]).astype(jnp.bfloat16)
            wz[UNK:] = jnp.where(lane_w[:128], fold[far + 2, :128], fold[far + 2, 128:]).astype(jnp.bfloat16)

            @pl.when(has_z)
            def _():
                send(wz, wr.at[pl.ds(0, UNK + 128)], 1, wsem.at[0], zdev)

            for j in (0, 2, 1):
                wy[j] = jnp.where(lane_w, fold[j], fold[BY + j]).astype(jnp.bfloat16)
            for side in range(2):
                @pl.when(has_y[side])
                def _():
                    send(wy.at[side * (BY - 1)], wr.at[pl.ds(UNK + 128 + UNK * (1 - side), UNK)], 5 + side, wsem.at[2 - side], ydev[side])
            whole(cp.at[pl.ds(0, BY)], lsem.at[5]).wait()
        for j in range(BY):
            cs[t, j] = product(near + j, odd)
        send(cs.at[t], cr.at[t], 9, csem.at[t], cdev)
        if t == ITERS - 1:
            for side in range(2):
                wait_if(has_y[side], (wr.at[pl.ds(UNK + 128 + UNK * side, UNK)], wsem.at[1 + side]))
                edge = wr[UNK + 128 + UNK * side:2 * UNK + 128 + UNK * side]
                part = jnp.where(lane_e, mm(ys[side, t, 0], edge), mm(ys[side, t, 1], edge))
                for p in range(PEERS):
                    gs[p, 2 + side] = part[4 * p:4 * p + 4]
            for side in range(2):
                @pl.when(has_y[side])
                def _():
                    for step in (6, 2, 5, 7, 1, 3, 4, 0):
                        send(gs.at[peers[step], pl.ds(2 + side, 1)], gr.at[pl.ds(16 + 8 * (1 - side) + step, 1)], 7 + side,
                             gsem.at[3 - side], {"bias": peers[step], **ydev[side]})

            send_z(t)
            send_y(t)
        if t == 0:
            whole(cp.at[pl.ds(0, len(inner))], lsem.at[7]).wait()
        for k in range(BLOCKS):
            i, j = divmod(k, BY)
            total = src[k].astype(jnp.float32)
            if i > 0:
                total = total - mm(a[k - BY], cp[4 * (k - BY)])
            if i < BX - 1:
                total = total - mm(a[k + BY], cp[4 * (k + BY) + 1])
            if j > 0:
                total = total - mm(a[k - 1], cp[4 * (k - 1) + 2])
            if j < BY - 1:
                total = total - mm(a[k + 1], cp[4 * (k + 1) + 3])
            acc[k] = total
        if t == 0:
            for j in range(BY):
                both[j] = mm(inv[far + j], cp[4 * (far + j) + 1 - odd]).astype(jnp.bfloat16)
            pl.semaphore_wait(rsem.at[0], 3)
            tell(1)
        whole(cr.at[t], csem.at[t]).wait()
        for j in range(BY):
            acc[near + j] = acc[near + j] - cr[t, j].astype(jnp.float32)
        if t == ITERS - 1:
            for j in range(BY):
                part = jnp.where(lane_e, mm(acc[j].astype(jnp.bfloat16), wy[j]), mm(acc[BY + j].astype(jnp.bfloat16), wy[j]))
                for p in range(PEERS):
                    gs[p, 4 + j] = part[4 * p:4 * p + 4]
            for step in (6, 2, 5, 7, 1, 3, 4):
                send(gs.at[peers[step], pl.ds(4, 3)], gr.at[pl.ds(32 + 3 * (step - 1), 3)], 10, gsem.at[0], {"bias": peers[step]})
        near_u = [acc[near + j] for j in range(BY)]
        a[near + 1] = mm(near_u[1].astype(jnp.bfloat16), inv[near + 1]).astype(jnp.bfloat16)
        for side in range(2):
            wait_if(has_y[side], (yr.at[side, t], ysem.at[side, t]))
        for side in range(2):
            j = side * (BY - 1)
            u = near_u[j] - jnp.where(has_y[side], yr[side, t, 1 - odd].astype(jnp.float32), 0.0)
            a[near + j] = mm(u.astype(jnp.bfloat16), inv[near + j]).astype(jnp.bfloat16)
        far_u = [acc[far + j] for j in range(BY)]
        for side in range(2):
            j = side * (BY - 1)
            far_u[j] = far_u[j] - jnp.where(has_y[side], yr[side, t, odd].astype(jnp.float32), 0.0)
        wait_if(has_z, (zr.at[t], zsem.at[t]))
        late = []
        for j in range(BY):
            u = far_u[j] - jnp.where(has_z, zr[t, j].astype(jnp.float32), 0.0)
            late.append(u.astype(jnp.bfloat16))
        if t < ITERS - 1:
            for j in range(BY):
                zs[t + 1, j] = mm(late[j], both[j]).astype(jnp.bfloat16)
            if t == 0:
                pl.semaphore_wait(rsem.at[1], 3)
            if t + 1 < ITERS - 1:
                send_z(t + 1)
            else:
                wait_if(has_z, (wr.at[pl.ds(0, UNK + 128)], wsem.at[0]))
                edge = wr[:UNK]
                tail = wr[UNK:UNK + 128]
                parts = [jnp.where(lane_e, mm(zs[t + 1, 0], edge), mm(zs[t + 1, 1], edge)),
                         mm(zs[t + 1, 2, :, :128], tail) + pltpu.roll(mm(zs[t + 1, 2, :, 128:], tail), 64, 1)]
                for m, part in enumerate(parts):
                    for p in range(PEERS):
                        gs[p, m] = part[4 * p:4 * p + 4]

                @pl.when(has_z)
                def _():
                    for step in (6, 2, 5, 7, 1, 3, 4, 0):
                        send(gs.at[peers[step], pl.ds(0, 2)], gr.at[pl.ds(2 * step, 2)], 2, gsem.at[1], {"bias": peers[step], **zdev})

        for j in range(BY):
            a[far + j] = mm(late[j], inv[far + j]).astype(jnp.bfloat16)

    adj_out[...] = a[...]
    whole(cs, ssem.at[9]).wait()
    totals = [gs[bias, 4 + j] for j in range(BY)]
    whole(gr.at[pl.ds(32, 3 * (PEERS - 1))], gsem.at[0]).wait()
    wait_if(has_z, (gr.at[pl.ds(0, 16)], gsem.at[1]))
    for side in range(2):
        wait_if(has_y[side], (gr.at[pl.ds(16 + 8 * side, 8)], gsem.at[2 + side]))
    for step in range(1, PEERS):
        for j in range(BY):
            totals[j] = totals[j] + gr[32 + 3 * (step - 1) + j]
    for side in range(2):
        part = gr[16 + 8 * side]
        for step in range(1, PEERS):
            part = part + gr[16 + 8 * side + step]
        j = side * (BY - 1)
        totals[j] = totals[j] - jnp.where(has_y[side], part, 0.0)
    pair, last = gr[0], gr[1]
    for step in range(1, PEERS):
        pair, last = pair + gr[2 * step], last + gr[2 * step + 1]
    turned = pltpu.roll(pair, 64, 1)
    half = lax.broadcasted_iota(jnp.int32, (4, 128), 1) // 64 == jnp.where(has_z, odd, -1)
    for j, part in enumerate((jnp.where(lane_g, pair, turned), jnp.where(lane_g, turned, pair),
                              jnp.where(lane_g, last, pltpu.roll(last, 64, 1)))):
        here = totals[j] - jnp.where(half, part, 0.0)
        other = pltpu.roll(here, 64, 1)
        for q in range(0, 4, 2):
            dop_out[j, 0:1, 64 * q:64 * q + 128] = jnp.where(lane_g[:1], here[q:q + 1], other[q + 1:q + 2])
            dop_out[j, 1:2, 64 * q:64 * q + 128] = jnp.where(lane_g[:1], other[q:q + 1], here[q + 1:q + 2])
    whole(gr.at[pl.ds(32, 3 * (PEERS - 1))], ssem.at[10]).wait()
    wait_if(has_z, (zs, ssem.at[0]), (wz, ssem.at[1]), (gr.at[pl.ds(0, 16)], ssem.at[2]))
    for side in range(2):
        wait_if(has_y[side], (ys.at[side], ssem.at[3 + side]), (wy.at[0], ssem.at[5 + side]),
                (gr.at[pl.ds(16, 8)], ssem.at[7 + side]))


def finish(adj_in, dop_in, adj_out, dop_out, sem):
    first = pltpu.make_async_copy(adj_in, adj_out, sem.at[0])
    second = pltpu.make_async_copy(dop_in, dop_out, sem.at[1])
    first.start()
    second.start()
    first.wait()
    second.wait()


def shards(source, inverse, coupling, sensitivity):
    src = source.reshape(BLOCKS, RHS, UNK)
    inv = inverse.reshape(BLOCKS, UNK, UNK)
    cp = coupling.reshape(BLOCKS * 4, UNK, UNK)
    sen = sensitivity.reshape(BX, BY, UNK).transpose(1, 0, 2)
    hbm = pl.BlockSpec(memory_space=pltpu.HBM)
    dma = pltpu.SemaphoreType.DMA
    adjoint, doping = pl.pallas_call(
        kernel,
        out_shape=(jax.ShapeDtypeStruct((BLOCKS, RHS, UNK), jnp.bfloat16),
                   jax.ShapeDtypeStruct((BY, BX, UNK), jnp.float32)),
        in_specs=[hbm] * 4,
        out_specs=(pl.BlockSpec(memory_space=pltpu.VMEM),) * 2,
        scratch_shapes=[
            pltpu.VMEM((BLOCKS, RHS, UNK), jnp.bfloat16),
            pltpu.VMEM((BLOCKS, UNK, UNK), jnp.bfloat16),
            pltpu.VMEM((BLOCKS * 4, UNK, UNK), jnp.bfloat16),
            pltpu.VMEM((BY, BX, UNK), jnp.float32),
            pltpu.VMEM((BLOCKS, RHS, UNK), jnp.bfloat16),
            pltpu.VMEM((BLOCKS, RHS, UNK), jnp.float32),
            pltpu.VMEM((ITERS, BY, RHS, UNK), jnp.bfloat16),
            pltpu.VMEM((ITERS, BY, RHS, UNK), jnp.bfloat16),
            pltpu.VMEM((ITERS, BY, RHS, UNK), jnp.bfloat16),
            pltpu.VMEM((ITERS, BY, RHS, UNK), jnp.bfloat16),
            pltpu.VMEM((2, ITERS, BX, RHS, UNK), jnp.bfloat16),
            pltpu.VMEM((2, ITERS, BX, RHS, UNK), jnp.bfloat16),
            pltpu.VMEM((BY, UNK, UNK), jnp.bfloat16),
            pltpu.VMEM((BLOCKS, UNK, 128), jnp.float32),
            pltpu.VMEM((UNK + 128, 128), jnp.bfloat16),
            pltpu.VMEM((BY, UNK, 128), jnp.bfloat16),
            pltpu.VMEM((3 * UNK + 128, 128), jnp.bfloat16),
            pltpu.VMEM((PEERS, 7, 4, 128), jnp.float32),
            pltpu.VMEM((16 + 16 + 3 * (PEERS - 1), 4, 128), jnp.float32),
            dma((8,)), dma((11,)), dma((ITERS,)), dma((ITERS,)), dma((2, ITERS)), dma((3,)), dma((4,)), pltpu.SemaphoreType.REGULAR((2,)),
        ],
        compiler_params=pltpu.CompilerParams(
            collective_id=0, has_side_effects=True, vmem_limit_bytes=40 * 1024 * 1024),
        cost_estimate=pl.CostEstimate(flops=403_000_000, bytes_accessed=4_200_000, transcendentals=0),
    )(*(pltpu.with_memory_space_constraint(x, pltpu.HBM) for x in (src, inv, cp, sen)))
    adjoint, doping = pl.pallas_call(
        finish,
        out_shape=(jax.ShapeDtypeStruct((BLOCKS, RHS, UNK), jnp.bfloat16),
                   jax.ShapeDtypeStruct((BY, BX, UNK), jnp.float32)),
        in_specs=[pl.BlockSpec(memory_space=pltpu.VMEM)] * 2,
        out_specs=(pl.BlockSpec(memory_space=pl.ANY),) * 2,
        scratch_shapes=[dma((2,))],
        compiler_params=pltpu.CompilerParams(vmem_limit_bytes=40 * 1024 * 1024),
    )(adjoint, doping)
    return (adjoint.reshape(1, BX, BY, RHS, UNK), doping.transpose(1, 0, 2))


def solution(mesh):
    placed = (
        P("bias", "gx", "gy", None, None),
        P("bias", "gx", "gy", None, None),
        P("bias", "gx", "gy", None, None, None),
        P("bias", "gx", "gy", None),
    )
    return jax.shard_map(
        shards,
        mesh=mesh,
        in_specs=placed,
        out_specs=(P("bias", "gx", "gy", None, None), P("gx", "gy", "bias")),
        check_vma=False,
    )
```

```python
import jax
import jax.numpy as jnp
from jax import lax
from jax.experimental import pallas as pl
from jax.experimental.pallas import tpu as pltpu
from jax.sharding import PartitionSpec as P

ITERS = 3
BX, BY = 2, 3
BLOCKS = BX * BY
RHS, UNK = 32, 256
PEERS = 8
MESH = pl.DeviceIdType.MESH


def mm(a, b):
    return jnp.dot(a, b, preferred_element_type=jnp.float32)


def whole(ref, sem):
    return pltpu.make_async_copy(ref, ref, sem)


def kernel(src_h, inv_h, cp_h, sen_h, adj_out, dop_out,
           src, inv, cp, sen, a, acc, zs, zr, cs, cr, ys, yr, both, fold, wz, wy, wr, gs, gr,
           lsem, ssem, zsem, csem, ysem, wsem, gsem, rsem):
    bias, gx, gy = lax.axis_index("bias"), lax.axis_index("gx"), lax.axis_index("gy")
    nb, nx, ny = lax.axis_size("bias"), lax.axis_size("gx"), lax.axis_size("gy")
    odd = lax.rem(gx, 2)
    far, near = odd * BY, (1 - odd) * BY
    zdev = {"gx": lax.rem(gx + nx + 2 * odd - 1, nx)}
    cdev = {"gx": gx + 1 - 2 * odd}
    ydev = ({"gy": lax.rem(gy + ny - 1, ny)}, {"gy": lax.rem(gy + 1, ny)})
    has_z = jnp.logical_and(gx + 2 * odd - 1 >= 0, gx + 2 * odd - 1 < nx)
    has_y = (gy > 0, gy < ny - 1)
    peers = [lax.rem(bias + step, nb) for step in range(PEERS)]

    ring = nb // 2
    place, half = lax.rem(bias, ring), bias - lax.rem(bias, ring)
    round_devs = ({"bias": half + lax.rem(place + 1, ring)}, {"bias": half + lax.rem(place + ring - 1, ring)},
                  {"bias": lax.rem(bias + ring, nb)})

    def tell(number):
        for dev in round_devs:
            pl.semaphore_signal(rsem.at[number], inc=1, device_id=dev, device_id_type=MESH)

    def load(from_ref, to_ref, sem):
        pltpu.make_async_copy(from_ref, to_ref, lsem.at[sem]).start()

    def load_tile(k, sem):
        load(cp_h.at[k], cp.at[k], sem)

    def product(k, d):
        return mm(a[k], cp[4 * k + d]).astype(jnp.bfloat16)

    def send(from_ref, to_ref, sent, landed, dev):
        pltpu.make_async_remote_copy(
            src_ref=from_ref, dst_ref=to_ref, send_sem=ssem.at[sent], recv_sem=landed,
            device_id=dev, device_id_type=MESH).start()

    def send_z(t):
        @pl.when(has_z)
        def _():
            send(zs.at[t], zr.at[t], 0, zsem.at[t], zdev)

    def send_y(t):
        for side in range(2):
            @pl.when(has_y[side])
            def _():
                send(ys.at[side, t], yr.at[1 - side, t], 3 + side, ysem.at[1 - side, t], ydev[side])

    def wait_if(there, *pairs):
        @pl.when(there)
        def _():
            for ref, sem in pairs:
                whole(ref, sem).wait()

    far_rows, near_rows = pl.ds(far, BY), pl.ds(near, BY)
    load(src_h, src, 0)
    load(inv_h.at[far_rows], inv.at[far_rows], 1)
    barrier = pltpu.get_barrier_semaphore()
    for dev, there in ((zdev, has_z), (ydev[0], has_y[0]), (ydev[1], has_y[1])):
        @pl.when(there)
        def _():
            pl.semaphore_signal(barrier, inc=1, device_id=dev, device_id_type=MESH)
    pl.semaphore_signal(barrier, inc=1, device_id=cdev, device_id_type=MESH)
    greeted = 4 + sum(there.astype(jnp.int32) for there in (has_z,) + has_y)
    for j in range(BY):
        load_tile(4 * (far + j) + 1 - odd, 2)
    for dev in round_devs:
        pl.semaphore_signal(barrier, inc=1, device_id=dev, device_id_type=MESH)
    load(inv_h.at[near_rows], inv.at[near_rows], 3)
    edge_y = [(i * BY + side * (BY - 1), 3 - side) for side in range(2) for i in range(BX)]
    for k, d in edge_y:
        load_tile(4 * k + d, 4)
    for j in range(BY):
        load_tile(4 * (near + j) + odd, 5)
    load(sen_h, sen, 6)

    @pl.when(jnp.logical_not(has_z))
    def _():
        zr[...] = jnp.zeros_like(zr)
        wr[:UNK + 128] = jnp.zeros((UNK + 128, 128), jnp.bfloat16)
        gr[:16] = jnp.zeros((16, 4, 128), jnp.float32)

    for side in range(2):
        @pl.when(jnp.logical_not(has_y[side]))
        def _():
            yr[side] = jnp.zeros((ITERS, BX, RHS, UNK), jnp.bfloat16)
            wr[UNK + 128 + UNK * side:2 * UNK + 128 + UNK * side] = jnp.zeros((UNK, 128), jnp.bfloat16)
            gr[16 + 8 * side:24 + 8 * side] = jnp.zeros((8, 4, 128), jnp.float32)

    whole(src, lsem.at[0]).wait()
    whole(inv.at[far_rows], lsem.at[1]).wait()
    for j in range(BY):
        a[far + j] = mm(src[far + j], inv[far + j]).astype(jnp.bfloat16)
    inner = [(j, 0) for j in range(BY)] + [(BY + j, 1) for j in range(BY)]
    inner += [(i * BY + j, 2) for i in range(BX) for j in range(BY - 1)]
    inner += [(i * BY + j, 3) for i in range(BX) for j in range(1, BY)]
    lane_w = lax.broadcasted_iota(jnp.int32, (UNK, 128), 1) < 64
    lane_e = lax.broadcasted_iota(jnp.int32, (RHS, 128), 1) < 64
    lane_g = lax.broadcasted_iota(jnp.int32, (4, 128), 1) < 64

    for t in range(ITERS):
        if t == 0:
            whole(cp.at[pl.ds(0, BY)], lsem.at[2]).wait()
        if t == 0:
            for j in range(BY):
                zs[0, j] = product(far + j, 1 - odd)
            pl.semaphore_wait(barrier, greeted)
            send_z(0)
            tell(0)
        if t == 0:
            for k, d in inner:
                load_tile(4 * k + d, 7)
            whole(inv.at[near_rows], lsem.at[3]).wait()
            for j in range(BY):
                a[near + j] = mm(src[near + j], inv[near + j]).astype(jnp.bfloat16)
            whole(cp.at[pl.ds(0, 2 * BX)], lsem.at[4]).wait()
        for side in range(2):
            for i in range(BX):
                k, d = edge_y[side * BX + i]
                ys[side, t, i] = product(k, d)
        if t < ITERS - 1:
            send_y(t)
        if t == 0:
            whole(sen, lsem.at[6]).wait()
            for k in range(BLOCKS):
                i, j = divmod(k, BY)
                h = inv[k].astype(jnp.float32) * sen[j, i:i + 1, :]
                h = h[:, :128] + h[:, 128:]
                fold[k] = h + pltpu.roll(h, 64, 1)
            wz[:UNK] = jnp.where(lane_w, fold[far], fold[far + 1]).astype(jnp.bfloat16)
            wz[UNK:] = jnp.where(lane_w[:128], fold[far + 2, :128], fold[far + 2, 128:]).astype(jnp.bfloat16)

            @pl.when(has_z)
            def _():
                send(wz, wr.at[pl.ds(0, UNK + 128)], 1, wsem.at[0], zdev)

            for j in (0, 2, 1):
                wy[j] = jnp.where(lane_w, fold[j], fold[BY + j]).astype(jnp.bfloat16)
            for side in range(2):
                @pl.when(has_y[side])
                def _():
                    send(wy.at[side * (BY - 1)], wr.at[pl.ds(UNK + 128 + UNK * (1 - side), UNK)], 5 + side, wsem.at[2 - side], ydev[side])
            whole(cp.at[pl.ds(0, BY)], lsem.at[5]).wait()
        for j in range(BY):
            cs[t, j] = product(near + j, odd)
        send(cs.at[t], cr.at[t], 9, csem.at[t], cdev)
        if t == ITERS - 1:
            for side in range(2):
                wait_if(has_y[side], (wr.at[pl.ds(UNK + 128 + UNK * side, UNK)], wsem.at[1 + side]))
                edge = wr[UNK + 128 + UNK * side:2 * UNK + 128 + UNK * side]
                part = jnp.where(lane_e, mm(ys[side, t, 0], edge), mm(ys[side, t, 1], edge))
                for p in range(PEERS):
                    gs[p, 2 + side] = part[4 * p:4 * p + 4]
            for side in range(2):
                @pl.when(has_y[side])
                def _():
                    for step in (6, 2, 5, 7, 1, 3, 4, 0):
                        send(gs.at[peers[step], pl.ds(2 + side, 1)], gr.at[pl.ds(16 + 8 * (1 - side) + step, 1)], 7 + side,
                             gsem.at[3 - side], {"bias": peers[step], **ydev[side]})

            send_z(t)
            send_y(t)
        if t == 0:
            whole(cp.at[pl.ds(0, len(inner))], lsem.at[7]).wait()
        for k in range(BLOCKS):
            i, j = divmod(k, BY)
            total = src[k].astype(jnp.float32)
            if i > 0:
                total = total - mm(a[k - BY], cp[4 * (k - BY)])
            if i < BX - 1:
                total = total - mm(a[k + BY], cp[4 * (k + BY) + 1])
            if j > 0:
                total = total - mm(a[k - 1], cp[4 * (k - 1) + 2])
            if j < BY - 1:
                total = total - mm(a[k + 1], cp[4 * (k + 1) + 3])
            acc[k] = total
        if t == 0:
            for j in range(BY):
                both[j] = mm(inv[far + j], cp[4 * (far + j) + 1 - odd]).astype(jnp.bfloat16)
            pl.semaphore_wait(rsem.at[0], 3)
            tell(1)
        whole(cr.at[t], csem.at[t]).wait()
        for j in range(BY):
            acc[near + j] = acc[near + j] - cr[t, j].astype(jnp.float32)
        if t == ITERS - 1:
            for j in range(BY):
                part = jnp.where(lane_e, mm(acc[j].astype(jnp.bfloat16), wy[j]), mm(acc[BY + j].astype(jnp.bfloat16), wy[j]))
                for p in range(PEERS):
                    gs[p, 4 + j] = part[4 * p:4 * p + 4]
            for step in (6, 2, 5, 7, 1, 3, 4):
                send(gs.at[peers[step], pl.ds(4, 3)], gr.at[pl.ds(32 + 3 * (step - 1), 3)], 10, gsem.at[0], {"bias": peers[step]})
        near_u = [acc[near + j] for j in range(BY)]
        a[near + 1] = mm(near_u[1].astype(jnp.bfloat16), inv[near + 1]).astype(jnp.bfloat16)
        for side in range(2):
            wait_if(has_y[side], (yr.at[side, t], ysem.at[side, t]))
        for side in range(2):
            j = side * (BY - 1)
            u = near_u[j] - yr[side, t, 1 - odd].astype(jnp.float32)
            a[near + j] = mm(u.astype(jnp.bfloat16), inv[near + j]).astype(jnp.bfloat16)
        far_u = [acc[far + j] for j in range(BY)]
        for side in range(2):
            j = side * (BY - 1)
            far_u[j] = far_u[j] - yr[side, t, odd].astype(jnp.float32)
        wait_if(has_z, (zr.at[t], zsem.at[t]))
        late = []
        for j in range(BY):
            u = far_u[j] - zr[t, j].astype(jnp.float32)
            late.append(u.astype(jnp.bfloat16))
        if t < ITERS - 1:
            for j in range(BY):
                zs[t + 1, j] = mm(late[j], both[j]).astype(jnp.bfloat16)
            if t == 0:
                pl.semaphore_wait(rsem.at[1], 3)
            if t + 1 < ITERS - 1:
                send_z(t + 1)
            else:
                wait_if(has_z, (wr.at[pl.ds(0, UNK + 128)], wsem.at[0]))
                edge = wr[:UNK]
                tail = wr[UNK:UNK + 128]
                parts = [jnp.where(lane_e, mm(zs[t + 1, 0], edge), mm(zs[t + 1, 1], edge)),
                         mm(zs[t + 1, 2, :, :128], tail) + pltpu.roll(mm(zs[t + 1, 2, :, 128:], tail), 64, 1)]
                for m, part in enumerate(parts):
                    for p in range(PEERS):
                        gs[p, m] = part[4 * p:4 * p + 4]

                @pl.when(has_z)
                def _():
                    for step in (6, 2, 5, 7, 1, 3, 4, 0):
                        send(gs.at[peers[step], pl.ds(0, 2)], gr.at[pl.ds(2 * step, 2)], 2, gsem.at[1], {"bias": peers[step], **zdev})

        for j in range(BY):
            a[far + j] = mm(late[j], inv[far + j]).astype(jnp.bfloat16)

    adj_out[...] = a[...]
    whole(cs, ssem.at[9]).wait()
    whole(gr.at[pl.ds(32, 3 * (PEERS - 1))], ssem.at[10]).wait()
    wait_if(has_z, (zs, ssem.at[0]), (wz, ssem.at[1]), (gr.at[pl.ds(0, 16)], ssem.at[2]))
    for side in range(2):
        wait_if(has_y[side], (ys.at[side], ssem.at[3 + side]), (wy.at[0], ssem.at[5 + side]),
                (gr.at[pl.ds(16, 8)], ssem.at[7 + side]))
    totals = [gs[bias, 4 + j] for j in range(BY)]
    whole(gr.at[pl.ds(32, 3 * (PEERS - 1))], gsem.at[0]).wait()
    wait_if(has_z, (gr.at[pl.ds(0, 16)], gsem.at[1]))
    for side in range(2):
        wait_if(has_y[side], (gr.at[pl.ds(16 + 8 * side, 8)], gsem.at[2 + side]))
    for step in range(1, PEERS):
        for j in range(BY):
            totals[j] = totals[j] + gr[32 + 3 * (step - 1) + j]
    for side in range(2):
        part = gr[16 + 8 * side]
        for step in range(1, PEERS):
            part = part + gr[16 + 8 * side + step]
        j = side * (BY - 1)
        totals[j] = totals[j] - part
    pair, last = gr[0], gr[1]
    for step in range(1, PEERS):
        pair, last = pair + gr[2 * step], last + gr[2 * step + 1]
    turned = pltpu.roll(pair, 64, 1)
    half = lax.broadcasted_iota(jnp.int32, (4, 128), 1) // 64 == odd
    for j, part in enumerate((jnp.where(lane_g, pair, turned), jnp.where(lane_g, turned, pair),
                              jnp.where(lane_g, last, pltpu.roll(last, 64, 1)))):
        here = totals[j] - jnp.where(half, part, 0.0)
        other = pltpu.roll(here, 64, 1)
        for q in range(0, 4, 2):
            dop_out[j, 0:1, 64 * q:64 * q + 128] = jnp.where(lane_g[:1], here[q:q + 1], other[q + 1:q + 2])
            dop_out[j, 1:2, 64 * q:64 * q + 128] = jnp.where(lane_g[:1], other[q:q + 1], here[q + 1:q + 2])


def finish(adj_in, dop_in, adj_out, dop_out, sem):
    first = pltpu.make_async_copy(adj_in, adj_out, sem.at[0])
    second = pltpu.make_async_copy(dop_in, dop_out, sem.at[1])
    first.start()
    second.start()
    first.wait()
    second.wait()


def shards(source, inverse, coupling, sensitivity):
    src = source.reshape(BLOCKS, RHS, UNK)
    inv = inverse.reshape(BLOCKS, UNK, UNK)
    cp = coupling.reshape(BLOCKS * 4, UNK, UNK)
    sen = sensitivity.reshape(BX, BY, UNK).transpose(1, 0, 2)
    hbm = pl.BlockSpec(memory_space=pltpu.HBM)
    dma = pltpu.SemaphoreType.DMA
    adjoint, doping = pl.pallas_call(
        kernel,
        out_shape=(jax.ShapeDtypeStruct((BLOCKS, RHS, UNK), jnp.bfloat16),
                   jax.ShapeDtypeStruct((BY, BX, UNK), jnp.float32)),
        in_specs=[hbm] * 4,
        out_specs=(pl.BlockSpec(memory_space=pltpu.VMEM),) * 2,
        scratch_shapes=[
            pltpu.VMEM((BLOCKS, RHS, UNK), jnp.bfloat16),
            pltpu.VMEM((BLOCKS, UNK, UNK), jnp.bfloat16),
            pltpu.VMEM((BLOCKS * 4, UNK, UNK), jnp.bfloat16),
            pltpu.VMEM((BY, BX, UNK), jnp.float32),
            pltpu.VMEM((BLOCKS, RHS, UNK), jnp.bfloat16),
            pltpu.VMEM((BLOCKS, RHS, UNK), jnp.float32),
            pltpu.VMEM((ITERS, BY, RHS, UNK), jnp.bfloat16),
            pltpu.VMEM((ITERS, BY, RHS, UNK), jnp.bfloat16),
            pltpu.VMEM((ITERS, BY, RHS, UNK), jnp.bfloat16),
            pltpu.VMEM((ITERS, BY, RHS, UNK), jnp.bfloat16),
            pltpu.VMEM((2, ITERS, BX, RHS, UNK), jnp.bfloat16),
            pltpu.VMEM((2, ITERS, BX, RHS, UNK), jnp.bfloat16),
            pltpu.VMEM((BY, UNK, UNK), jnp.bfloat16),
            pltpu.VMEM((BLOCKS, UNK, 128), jnp.float32),
            pltpu.VMEM((UNK + 128, 128), jnp.bfloat16),
            pltpu.VMEM((BY, UNK, 128), jnp.bfloat16),
            pltpu.VMEM((3 * UNK + 128, 128), jnp.bfloat16),
            pltpu.VMEM((PEERS, 7, 4, 128), jnp.float32),
            pltpu.VMEM((16 + 16 + 3 * (PEERS - 1), 4, 128), jnp.float32),
            dma((8,)), dma((11,)), dma((ITERS,)), dma((ITERS,)), dma((2, ITERS)), dma((3,)), dma((4,)), pltpu.SemaphoreType.REGULAR((2,)),
        ],
        compiler_params=pltpu.CompilerParams(
            collective_id=0, has_side_effects=True, vmem_limit_bytes=40 * 1024 * 1024),
        cost_estimate=pl.CostEstimate(flops=403_000_000, bytes_accessed=4_200_000, transcendentals=0),
    )(*(pltpu.with_memory_space_constraint(x, pltpu.HBM) for x in (src, inv, cp, sen)))
    adjoint, doping = pl.pallas_call(
        finish,
        out_shape=(jax.ShapeDtypeStruct((BLOCKS, RHS, UNK), jnp.bfloat16),
                   jax.ShapeDtypeStruct((BY, BX, UNK), jnp.float32)),
        in_specs=[pl.BlockSpec(memory_space=pltpu.VMEM)] * 2,
        out_specs=(pl.BlockSpec(memory_space=pl.ANY),) * 2,
        scratch_shapes=[dma((2,))],
        compiler_params=pltpu.CompilerParams(vmem_limit_bytes=40 * 1024 * 1024),
    )(adjoint, doping)
    return (adjoint.reshape(1, BX, BY, RHS, UNK), doping.transpose(1, 0, 2))


def solution(mesh):
    placed = (
        P("bias", "gx", "gy", None, None),
        P("bias", "gx", "gy", None, None),
        P("bias", "gx", "gy", None, None, None),
        P("bias", "gx", "gy", None),
    )
    return jax.shard_map(
        shards,
        mesh=mesh,
        in_specs=placed,
        out_specs=(P("bias", "gx", "gy", None, None), P("gx", "gy", "bias")),
        check_vma=False,
    )
```

```python
import jax
import jax.numpy as jnp
from jax import lax
from jax.experimental import pallas as pl
from jax.experimental.pallas import tpu as pltpu
from jax.sharding import PartitionSpec as P

ITERS = 3
BX, BY = 2, 3
BLOCKS = BX * BY
RHS, UNK = 32, 256
PEERS = 8
MESH = pl.DeviceIdType.MESH


def mm(a, b):
    return jnp.dot(a, b, preferred_element_type=jnp.float32)


def whole(ref, sem):
    return pltpu.make_async_copy(ref, ref, sem)


def kernel(src_h, inv_h, cp_h, sen_h, adj_out, dop_out,
           src, inv, cp, sen, a, acc, zs, zr, cs, cr, ys, yr, both, fold, wz, wy, wr, gs, gr,
           lsem, ssem, zsem, csem, ysem, wsem, gsem, rsem):
    bias, gx, gy = lax.axis_index("bias"), lax.axis_index("gx"), lax.axis_index("gy")
    nb, nx, ny = lax.axis_size("bias"), lax.axis_size("gx"), lax.axis_size("gy")
    odd = lax.rem(gx, 2)
    far, near = odd * BY, (1 - odd) * BY
    zdev = {"gx": lax.rem(gx + nx + 2 * odd - 1, nx)}
    cdev = {"gx": gx + 1 - 2 * odd}
    ydev = ({"gy": lax.rem(gy + ny - 1, ny)}, {"gy": lax.rem(gy + 1, ny)})
    has_z = jnp.logical_and(gx + 2 * odd - 1 >= 0, gx + 2 * odd - 1 < nx)
    has_y = (gy > 0, gy < ny - 1)
    peers = [lax.rem(bias + step, nb) for step in range(PEERS)]

    ring = nb // 2
    place, half = lax.rem(bias, ring), bias - lax.rem(bias, ring)
    round_devs = ({"bias": half + lax.rem(place + 1, ring)}, {"bias": half + lax.rem(place + ring - 1, ring)},
                  {"bias": lax.rem(bias + ring, nb)})

    def tell(number):
        for dev in round_devs:
            pl.semaphore_signal(rsem.at[number], inc=1, device_id=dev, device_id_type=MESH)

    def load(from_ref, to_ref, sem):
        pltpu.make_async_copy(from_ref, to_ref, lsem.at[sem]).start()

    def load_tile(k, sem):
        load(cp_h.at[k], cp.at[k], sem)

    def product(k, d):
        return mm(a[k], cp[4 * k + d]).astype(jnp.bfloat16)

    def send(from_ref, to_ref, sent, landed, dev):
        pltpu.make_async_remote_copy(
            src_ref=from_ref, dst_ref=to_ref, send_sem=ssem.at[sent], recv_sem=landed,
            device_id=dev, device_id_type=MESH).start()

    def send_z(t):
        @pl.when(has_z)
        def _():
            send(zs.at[t], zr.at[t], 0, zsem.at[t], zdev)

    def send_y(t):
        for side in range(2):
            @pl.when(has_y[side])
            def _():
                send(ys.at[side, t], yr.at[1 - side, t], 3 + side, ysem.at[1 - side, t], ydev[side])

    def wait_if(there, *pairs):
        @pl.when(there)
        def _():
            for ref, sem in pairs:
                whole(ref, sem).wait()

    far_rows, near_rows = pl.ds(far, BY), pl.ds(near, BY)
    load(src_h, src, 0)
    load(inv_h.at[far_rows], inv.at[far_rows], 1)
    barrier = pltpu.get_barrier_semaphore()
    for dev, there in ((zdev, has_z), (ydev[0], has_y[0]), (ydev[1], has_y[1])):
        @pl.when(there)
        def _():
            pl.semaphore_signal(barrier, inc=1, device_id=dev, device_id_type=MESH)
    pl.semaphore_signal(barrier, inc=1, device_id=cdev, device_id_type=MESH)
    greeted = 4 + sum(there.astype(jnp.int32) for there in (has_z,) + has_y)
    for j in range(BY):
        load_tile(4 * (far + j) + 1 - odd, 2)
    for dev in round_devs:
        pl.semaphore_signal(barrier, inc=1, device_id=dev, device_id_type=MESH)
    load(inv_h.at[near_rows], inv.at[near_rows], 3)
    edge_y = [(i * BY + side * (BY - 1), 3 - side) for side in range(2) for i in range(BX)]
    for k, d in edge_y:
        load_tile(4 * k + d, 4)
    for j in range(BY):
        load_tile(4 * (near + j) + odd, 5)
    load(sen_h, sen, 6)

    @pl.when(jnp.logical_not(has_z))
    def _():
        zr[...] = jnp.zeros_like(zr)
        wr[:UNK + 128] = jnp.zeros((UNK + 128, 128), jnp.bfloat16)
        gr[:16] = jnp.zeros((16, 4, 128), jnp.float32)

    for side in range(2):
        @pl.when(jnp.logical_not(has_y[side]))
        def _():
            yr[side] = jnp.zeros((ITERS, BX, RHS, UNK), jnp.bfloat16)
            wr[UNK + 128 + UNK * side:2 * UNK + 128 + UNK * side] = jnp.zeros((UNK, 128), jnp.bfloat16)
            gr[16 + 8 * side:24 + 8 * side] = jnp.zeros((8, 4, 128), jnp.float32)

    whole(src, lsem.at[0]).wait()
    whole(inv.at[far_rows], lsem.at[1]).wait()
    for j in range(BY):
        a[far + j] = mm(src[far + j], inv[far + j]).astype(jnp.bfloat16)
    inner = [(j, 0) for j in range(BY)] + [(BY + j, 1) for j in range(BY)]
    inner += [(i * BY + j, 2) for i in range(BX) for j in range(BY - 1)]
    inner += [(i * BY + j, 3) for i in range(BX) for j in range(1, BY)]
    lane_w = lax.broadcasted_iota(jnp.int32, (UNK, 128), 1) < 64
    lane_e = lax.broadcasted_iota(jnp.int32, (RHS, 128), 1) < 64
    lane_g = lax.broadcasted_iota(jnp.int32, (4, 128), 1) < 64

    for t in range(ITERS):
        if t == 0:
            whole(cp.at[pl.ds(0, BY)], lsem.at[2]).wait()
        if t == 0:
            for j in range(BY):
                zs[0, j] = product(far + j, 1 - odd)
            pl.semaphore_wait(barrier, greeted)
            send_z(0)
            tell(0)
        if t == 0:
            for k, d in inner:
                load_tile(4 * k + d, 7)
            whole(inv.at[near_rows], lsem.at[3]).wait()
            for j in range(BY):
                a[near + j] = mm(src[near + j], inv[near + j]).astype(jnp.bfloat16)
            whole(cp.at[pl.ds(0, 2 * BX)], lsem.at[4]).wait()
        if t == ITERS - 1:
            for j in range(BY):
                cs[t, j] = product(near + j, odd)
            send(cs.at[t], cr.at[t], 9, csem.at[t], cdev)
        for side in range(2):
            for i in range(BX):
                k, d = edge_y[side * BX + i]
                ys[side, t, i] = product(k, d)
        if t < ITERS - 1:
            send_y(t)
        if t == 0:
            whole(sen, lsem.at[6]).wait()
            for k in range(BLOCKS):
                i, j = divmod(k, BY)
                h = inv[k].astype(jnp.float32) * sen[j, i:i + 1, :]
                h = h[:, :128] + h[:, 128:]
                fold[k] = h + pltpu.roll(h, 64, 1)
            wz[:UNK] = jnp.where(lane_w, fold[far], fold[far + 1]).astype(jnp.bfloat16)
            wz[UNK:] = jnp.where(lane_w[:128], fold[far + 2, :128], fold[far + 2, 128:]).astype(jnp.bfloat16)

            @pl.when(has_z)
            def _():
                send(wz, wr.at[pl.ds(0, UNK + 128)], 1, wsem.at[0], zdev)

            for j in (0, 2, 1):
                wy[j] = jnp.where(lane_w, fold[j], fold[BY + j]).astype(jnp.bfloat16)
            for side in range(2):
                @pl.when(has_y[side])
                def _():
                    send(wy.at[side * (BY - 1)], wr.at[pl.ds(UNK + 128 + UNK * (1 - side), UNK)], 5 + side, wsem.at[2 - side], ydev[side])
            whole(cp.at[pl.ds(0, BY)], lsem.at[5]).wait()
        if t < ITERS - 1:
            for j in range(BY):
                cs[t, j] = product(near + j, odd)
            send(cs.at[t], cr.at[t], 9, csem.at[t], cdev)
        if t == ITERS - 1:
            for side in range(2):
                wait_if(has_y[side], (wr.at[pl.ds(UNK + 128 + UNK * side, UNK)], wsem.at[1 + side]))
                edge = wr[UNK + 128 + UNK * side:2 * UNK + 128 + UNK * side]
                part = jnp.where(lane_e, mm(ys[side, t, 0], edge), mm(ys[side, t, 1], edge))
                for p in range(PEERS):
                    gs[p, 2 + side] = part[4 * p:4 * p + 4]
            for side in range(2):
                @pl.when(has_y[side])
                def _():
                    for step in (6, 2, 5, 7, 1, 3, 4, 0):
                        send(gs.at[peers[step], pl.ds(2 + side, 1)], gr.at[pl.ds(16 + 8 * (1 - side) + step, 1)], 7 + side,
                             gsem.at[3 - side], {"bias": peers[step], **ydev[side]})

            send_z(t)
            send_y(t)
        if t == 0:
            whole(cp.at[pl.ds(0, len(inner))], lsem.at[7]).wait()
        for k in range(BLOCKS):
            i, j = divmod(k, BY)
            total = src[k].astype(jnp.float32)
            if i > 0:
                total = total - mm(a[k - BY], cp[4 * (k - BY)])
            if i < BX - 1:
                total = total - mm(a[k + BY], cp[4 * (k + BY) + 1])
            if j > 0:
                total = total - mm(a[k - 1], cp[4 * (k - 1) + 2])
            if j < BY - 1:
                total = total - mm(a[k + 1], cp[4 * (k + 1) + 3])
            acc[k] = total
        if t == 0:
            for j in range(BY):
                both[j] = mm(inv[far + j], cp[4 * (far + j) + 1 - odd]).astype(jnp.bfloat16)
            pl.semaphore_wait(rsem.at[0], 3)
            tell(1)
        whole(cr.at[t], csem.at[t]).wait()
        for j in range(BY):
            acc[near + j] = acc[near + j] - cr[t, j].astype(jnp.float32)
        if t == ITERS - 1:
            for j in range(BY):
                part = jnp.where(lane_e, mm(acc[j].astype(jnp.bfloat16), wy[j]), mm(acc[BY + j].astype(jnp.bfloat16), wy[j]))
                for p in range(PEERS):
                    gs[p, 4 + j] = part[4 * p:4 * p + 4]
            for step in (6, 2, 5, 7, 1, 3, 4):
                send(gs.at[peers[step], pl.ds(4, 3)], gr.at[pl.ds(32 + 3 * (step - 1), 3)], 10, gsem.at[0], {"bias": peers[step]})
        near_u = [acc[near + j] for j in range(BY)]
        a[near + 1] = mm(near_u[1].astype(jnp.bfloat16), inv[near + 1]).astype(jnp.bfloat16)
        for side in range(2):
            wait_if(has_y[side], (yr.at[side, t], ysem.at[side, t]))
        for side in range(2):
            j = side * (BY - 1)
            u = near_u[j] - jnp.where(has_y[side], yr[side, t, 1 - odd].astype(jnp.float32), 0.0)
            a[near + j] = mm(u.astype(jnp.bfloat16), inv[near + j]).astype(jnp.bfloat16)
        far_u = [acc[far + j] for j in range(BY)]
        for side in range(2):
            j = side * (BY - 1)
            far_u[j] = far_u[j] - jnp.where(has_y[side], yr[side, t, odd].astype(jnp.float32), 0.0)
        wait_if(has_z, (zr.at[t], zsem.at[t]))
        late = []
        for j in range(BY):
            u = far_u[j] - jnp.where(has_z, zr[t, j].astype(jnp.float32), 0.0)
            late.append(u.astype(jnp.bfloat16))
        if t < ITERS - 1:
            for j in range(BY):
                zs[t + 1, j] = mm(late[j], both[j]).astype(jnp.bfloat16)
            if t == 0:
                pl.semaphore_wait(rsem.at[1], 3)
            if t + 1 < ITERS - 1:
                send_z(t + 1)
            else:
                wait_if(has_z, (wr.at[pl.ds(0, UNK + 128)], wsem.at[0]))
                edge = wr[:UNK]
                tail = wr[UNK:UNK + 128]
                parts = [jnp.where(lane_e, mm(zs[t + 1, 0], edge), mm(zs[t + 1, 1], edge)),
                         mm(zs[t + 1, 2, :, :128], tail) + pltpu.roll(mm(zs[t + 1, 2, :, 128:], tail), 64, 1)]
                for m, part in enumerate(parts):
                    for p in range(PEERS):
                        gs[p, m] = part[4 * p:4 * p + 4]

                @pl.when(has_z)
                def _():
                    for step in (6, 2, 5, 7, 1, 3, 4, 0):
                        send(gs.at[peers[step], pl.ds(0, 2)], gr.at[pl.ds(2 * step, 2)], 2, gsem.at[1], {"bias": peers[step], **zdev})

        for j in range(BY):
            a[far + j] = mm(late[j], inv[far + j]).astype(jnp.bfloat16)

    adj_out[...] = a[...]
    whole(cs, ssem.at[9]).wait()
    totals = [gs[bias, 4 + j] for j in range(BY)]
    whole(gr.at[pl.ds(32, 3 * (PEERS - 1))], gsem.at[0]).wait()
    wait_if(has_z, (gr.at[pl.ds(0, 16)], gsem.at[1]))
    for side in range(2):
        wait_if(has_y[side], (gr.at[pl.ds(16 + 8 * side, 8)], gsem.at[2 + side]))
    for step in range(1, PEERS):
        for j in range(BY):
            totals[j] = totals[j] + gr[32 + 3 * (step - 1) + j]
    for side in range(2):
        part = gr[16 + 8 * side]
        for step in range(1, PEERS):
            part = part + gr[16 + 8 * side + step]
        j = side * (BY - 1)
        totals[j] = totals[j] - jnp.where(has_y[side], part, 0.0)
    pair, last = gr[0], gr[1]
    for step in range(1, PEERS):
        pair, last = pair + gr[2 * step], last + gr[2 * step + 1]
    turned = pltpu.roll(pair, 64, 1)
    half = lax.broadcasted_iota(jnp.int32, (4, 128), 1) // 64 == jnp.where(has_z, odd, -1)
    for j, part in enumerate((jnp.where(lane_g, pair, turned), jnp.where(lane_g, turned, pair),
                              jnp.where(lane_g, last, pltpu.roll(last, 64, 1)))):
        here = totals[j] - jnp.where(half, part, 0.0)
        other = pltpu.roll(here, 64, 1)
        for q in range(0, 4, 2):
            dop_out[j, 0:1, 64 * q:64 * q + 128] = jnp.where(lane_g[:1], here[q:q + 1], other[q + 1:q + 2])
            dop_out[j, 1:2, 64 * q:64 * q + 128] = jnp.where(lane_g[:1], other[q:q + 1], here[q + 1:q + 2])
    whole(gr.at[pl.ds(32, 3 * (PEERS - 1))], ssem.at[10]).wait()
    wait_if(has_z, (zs, ssem.at[0]), (wz, ssem.at[1]), (gr.at[pl.ds(0, 16)], ssem.at[2]))
    for side in range(2):
        wait_if(has_y[side], (ys.at[side], ssem.at[3 + side]), (wy.at[0], ssem.at[5 + side]),
                (gr.at[pl.ds(16, 8)], ssem.at[7 + side]))


def finish(adj_in, dop_in, adj_out, dop_out, sem):
    first = pltpu.make_async_copy(adj_in, adj_out, sem.at[0])
    second = pltpu.make_async_copy(dop_in, dop_out, sem.at[1])
    first.start()
    second.start()
    first.wait()
    second.wait()


def shards(source, inverse, coupling, sensitivity):
    src = source.reshape(BLOCKS, RHS, UNK)
    inv = inverse.reshape(BLOCKS, UNK, UNK)
    cp = coupling.reshape(BLOCKS * 4, UNK, UNK)
    sen = sensitivity.reshape(BX, BY, UNK).transpose(1, 0, 2)
    hbm = pl.BlockSpec(memory_space=pltpu.HBM)
    dma = pltpu.SemaphoreType.DMA
    adjoint, doping = pl.pallas_call(
        kernel,
        out_shape=(jax.ShapeDtypeStruct((BLOCKS, RHS, UNK), jnp.bfloat16),
                   jax.ShapeDtypeStruct((BY, BX, UNK), jnp.float32)),
        in_specs=[hbm] * 4,
        out_specs=(pl.BlockSpec(memory_space=pltpu.VMEM),) * 2,
        scratch_shapes=[
            pltpu.VMEM((BLOCKS, RHS, UNK), jnp.bfloat16),
            pltpu.VMEM((BLOCKS, UNK, UNK), jnp.bfloat16),
            pltpu.VMEM((BLOCKS * 4, UNK, UNK), jnp.bfloat16),
            pltpu.VMEM((BY, BX, UNK), jnp.float32),
            pltpu.VMEM((BLOCKS, RHS, UNK), jnp.bfloat16),
            pltpu.VMEM((BLOCKS, RHS, UNK), jnp.float32),
            pltpu.VMEM((ITERS, BY, RHS, UNK), jnp.bfloat16),
            pltpu.VMEM((ITERS, BY, RHS, UNK), jnp.bfloat16),
            pltpu.VMEM((ITERS, BY, RHS, UNK), jnp.bfloat16),
            pltpu.VMEM((ITERS, BY, RHS, UNK), jnp.bfloat16),
            pltpu.VMEM((2, ITERS, BX, RHS, UNK), jnp.bfloat16),
            pltpu.VMEM((2, ITERS, BX, RHS, UNK), jnp.bfloat16),
            pltpu.VMEM((BY, UNK, UNK), jnp.bfloat16),
            pltpu.VMEM((BLOCKS, UNK, 128), jnp.float32),
            pltpu.VMEM((UNK + 128, 128), jnp.bfloat16),
            pltpu.VMEM((BY, UNK, 128), jnp.bfloat16),
            pltpu.VMEM((3 * UNK + 128, 128), jnp.bfloat16),
            pltpu.VMEM((PEERS, 7, 4, 128), jnp.float32),
            pltpu.VMEM((16 + 16 + 3 * (PEERS - 1), 4, 128), jnp.float32),
            dma((8,)), dma((11,)), dma((ITERS,)), dma((ITERS,)), dma((2, ITERS)), dma((3,)), dma((4,)), pltpu.SemaphoreType.REGULAR((2,)),
        ],
        compiler_params=pltpu.CompilerParams(
            collective_id=0, has_side_effects=True, vmem_limit_bytes=40 * 1024 * 1024),
        cost_estimate=pl.CostEstimate(flops=403_000_000, bytes_accessed=4_200_000, transcendentals=0),
    )(*(pltpu.with_memory_space_constraint(x, pltpu.HBM) for x in (src, inv, cp, sen)))
    adjoint, doping = pl.pallas_call(
        finish,
        out_shape=(jax.ShapeDtypeStruct((BLOCKS, RHS, UNK), jnp.bfloat16),
                   jax.ShapeDtypeStruct((BY, BX, UNK), jnp.float32)),
        in_specs=[pl.BlockSpec(memory_space=pltpu.VMEM)] * 2,
        out_specs=(pl.BlockSpec(memory_space=pl.ANY),) * 2,
        scratch_shapes=[dma((2,))],
        compiler_params=pltpu.CompilerParams(vmem_limit_bytes=40 * 1024 * 1024),
    )(adjoint, doping)
    return (adjoint.reshape(1, BX, BY, RHS, UNK), doping.transpose(1, 0, 2))


def solution(mesh):
    placed = (
        P("bias", "gx", "gy", None, None),
        P("bias", "gx", "gy", None, None),
        P("bias", "gx", "gy", None, None, None),
        P("bias", "gx", "gy", None),
    )
    return jax.shard_map(
        shards,
        mesh=mesh,
        in_specs=placed,
        out_specs=(P("bias", "gx", "gy", None, None), P("gx", "gy", "bias")),
        check_vma=False,
    )
```
